128 devices in a mesh: ia: 16 (over z, x_hi, core), ja: 8 (over y, x_lo).
Axes of the slice: x: 4 (x_hi: 2, x_lo: 2; x = x_hi * 2 + x_lo), y: 4, z: 4, core: 2. Of those that a mesh axis runs over, the one named last changes fastest.
Arguments:
- heat_centre_value: float32 [16, 1024, 2048], P(None, 'ja', 'ia'), may hold values from -6 to 6
- saltiness_centre: float32 [16, 1024, 2048], P(None, 'ja', 'ia'), may hold values from -6 to 6
- easting_transport_ratio: float32 [16, 1024, 2048], P(None, 'ja', 'ia'), may hold values from -0.25 to 0.25
- northing_transport_ratio: float32 [16, 1024, 2048], P(None, 'ja', 'ia'), may hold values from -0.25 to 0.25
- sinking_transport_ratio: float32 [16, 1024, 2048], P(None, 'ja', 'ia'), may hold values from -0.15 to 0.15
- spreading_number: float32 [16, 1024, 2048], P(None, 'ja', 'ia'), may hold values from 0.01 to 0.08
- seawater_indicator: int32 [1024, 2048], P('ja', 'ia'), may hold values 0 or 1
- bottom_water_layer: int32 [1024, 2048], P('ja', 'ia'), may hold values from 1 to 16
Outputs:
- temperature_new: float32 [16, 1024, 2048], P(None, 'ja', 'ia')
- salinity_new: float32 [16, 1024, 2048], P(None, 'ja', 'ia')
The draws below stay inside these ranges and needn't reach their ends.
All inputs are finite; a program needn't handle non-finite values. No bound on the sum of `seawater_indicator` on one device may be relied on, other than what follows from the above.
Results may differ from the reference program's by a relative error of at most 0.0003.
Values sent between devices are 32-bit elements; how exact they have to be, the bound alone decides.
A program may use at most 256 MiB of HBM per device.

```python
import math
import jax
import jax.numpy as jnp
from jax import lax

DEPTH_LAYERS = 16
LONGITUDE_POINTS = 2048
LATITUDE_POINTS = 1024


def touch_ends(drawn, rng, low, high):
    place = [jax.random.randint(jax.random.fold_in(rng, axis), (), 0, length) for axis, length in enumerate(drawn.shape)]
    longest = drawn.shape.index(max(drawn.shape))
    next_to = place[:longest] + [(place[longest] + 1) % drawn.shape[longest]] + place[longest + 1:]
    return drawn.at[tuple(place)].set(low).at[tuple(next_to)].set(high)


def shard_levels(key, extent, split, low, top_value):
    level = 1.0
    for position, shards_of in split:
        steps = jax.random.uniform(jax.random.fold_in(jax.random.fold_in(key, 6), position), (shards_of,), jnp.float32, low / len(split), top_value / len(split))
        level = level * jnp.repeat(jnp.exp(steps), extent[position] // shards_of).reshape((-1,) + (1,) * (len(extent) - 1 - position))
    return level


def bell_draw(rng, dims, spread, reach, pieces=(), held_as=jnp.bfloat16):
    array = jax.random.normal(rng, dims, jnp.float32) * spread
    if len(pieces) > 0:
        array = shard_levels(rng, dims, pieces, -0.22, 0.18) * array
    return jnp.clip(array, min=-reach, max=reach).astype(held_as)


def setup_inputs(seed: int = 0) -> dict:
    streams_of = jax.random.split(jax.random.key(seed), 9)
    return {
        "heat_centre_value": bell_draw(streams_of[0], (DEPTH_LAYERS, LATITUDE_POINTS, LONGITUDE_POINTS), 1.0, 6.0, ((1, 8), (2, 16)), jnp.float32),
        "saltiness_centre": bell_draw(streams_of[1], (DEPTH_LAYERS, LATITUDE_POINTS, LONGITUDE_POINTS), 1.0, 6.0, ((1, 8), (2, 16)), jnp.float32),
        "easting_transport_ratio": jnp.clip(jax.random.uniform(streams_of[2], (DEPTH_LAYERS, LATITUDE_POINTS, LONGITUDE_POINTS), jnp.float32, -0.25, 0.25) * shard_levels(streams_of[2], (DEPTH_LAYERS, LATITUDE_POINTS, LONGITUDE_POINTS), ((1, 8), (2, 16)), -0.4, 0.0), -0.25, 0.25),
        "northing_transport_ratio": jnp.clip(jax.random.uniform(streams_of[3], (DEPTH_LAYERS, LATITUDE_POINTS, LONGITUDE_POINTS), jnp.float32, -0.25, 0.25) * shard_levels(streams_of[3], (DEPTH_LAYERS, LATITUDE_POINTS, LONGITUDE_POINTS), ((1, 8), (2, 16)), -0.4, 0.0), -0.25, 0.25),
        "sinking_transport_ratio": jnp.clip(jax.random.uniform(streams_of[4], (DEPTH_LAYERS, LATITUDE_POINTS, LONGITUDE_POINTS), jnp.float32, -0.15, 0.15) * shard_levels(streams_of[4], (DEPTH_LAYERS, LATITUDE_POINTS, LONGITUDE_POINTS), ((1, 8), (2, 16)), -0.4, 0.0), -0.15, 0.15),
        "spreading_number": jnp.clip(jnp.exp(math.log(0.08) - 2.0794415 * jax.random.uniform(streams_of[5], (DEPTH_LAYERS, LATITUDE_POINTS, LONGITUDE_POINTS), jnp.float32) ** shard_levels(streams_of[5], (DEPTH_LAYERS, LATITUDE_POINTS, LONGITUDE_POINTS), ((1, 8), (2, 16)), -0.2, 0.2)), 0.01, 0.08),
        "seawater_indicator": touch_ends((jax.random.randint(streams_of[6], (LATITUDE_POINTS, LONGITUDE_POINTS), 0, 5) < 4).astype(jnp.int32), jax.random.fold_in(streams_of[6], 1), 0, 1),
        "bottom_water_layer": touch_ends(jax.random.randint(streams_of[7], (LATITUDE_POINTS, LONGITUDE_POINTS), 1, DEPTH_LAYERS + 1), jax.random.fold_in(streams_of[7], 1), 1, DEPTH_LAYERS).astype(jnp.int32),
    }


def slice_edges(x, low_cut, high_cut, direction):
    dim_index = x.ndim + direction
    return lax.slice_in_dim(x, low_cut, x.shape[dim_index] - high_cut, axis=dim_index)


def limited(left, right):
    magnitude = jnp.minimum(jnp.minimum(2.0 * jnp.abs(left), 0.5 * jnp.abs(left + right)), 2.0 * jnp.abs(right))
    return jnp.where(left * right > 0, jnp.sign(left) * magnitude, 0.0 * magnitude)


def divergence(q, speeds_all, mixing, wet_cells, direction):
    open_faces = slice_edges(wet_cells, 0, 1, direction) * slice_edges(wet_cells, 1, 0, direction)
    jumps = (slice_edges(q, 1, 0, direction) - slice_edges(q, 0, 1, direction)) * open_faces
    slopes = limited(slice_edges(jumps, 0, 1, direction), slice_edges(jumps, 1, 0, direction))
    near_cell = slice_edges(q, 1, 2, direction)
    far_cell = slice_edges(q, 2, 1, direction)
    near_slope = slice_edges(slopes, 0, 1, direction)
    far_slope = slice_edges(slopes, 1, 0, direction)
    speeds = slice_edges(speeds_all, 1, 2, direction)
    face_value = jnp.where(speeds > 0, near_cell + 0.5 * (1.0 - speeds) * near_slope, far_cell - 0.5 * (1.0 + speeds) * far_slope)
    face_kappa = 0.5 * (slice_edges(mixing, 1, 2, direction) + slice_edges(mixing, 2, 1, direction))
    fluxes = (speeds * face_value - face_kappa * (far_cell - near_cell)) * slice_edges(open_faces, 1, 1, direction)
    return slice_edges(fluxes, 1, 0, direction) - slice_edges(fluxes, 0, 1, direction)


def advance(q, easting_transport_ratio, northing_transport_ratio, sinking_transport_ratio, spreading_number, floor_depth):
    level_index = jnp.arange(q.shape[1]).astype(jnp.float32)[:, None, None]
    wet_cells = (level_index < floor_depth[None]).astype(jnp.float32)
    zonal_div = divergence(q, easting_transport_ratio, spreading_number, wet_cells, -1)[..., 2:-2, :]
    north_div = divergence(q, northing_transport_ratio, spreading_number, wet_cells, -2)[..., 2:-2]
    padded = jnp.pad(q, ((0, 0), (2, 2), (0, 0), (0, 0)))
    padded_speed = jnp.pad(sinking_transport_ratio, ((2, 2), (0, 0), (0, 0)))
    padded_wet = jnp.pad(wet_cells, ((2, 2), (0, 0), (0, 0)))
    no_mixing = jnp.zeros_like(padded_speed)
    vertical_div = divergence(padded, padded_speed, no_mixing, padded_wet, -3)[..., 2:-2, 2:-2]
    center = q[..., 2:-2, 2:-2]
    return (center - zonal_div - north_div - vertical_div) * wet_cells[:, 2:-2, 2:-2]


def extend_grid(x, m, fold_sign):
    zonal_ext = jnp.concatenate([x[..., -m:], x, x[..., :m]], axis=-1)
    row_count = x.shape[-2]
    south_pad = jnp.zeros_like(zonal_ext[..., :m, :])
    north_pad = zonal_ext[..., row_count - m:, :][..., ::-1, ::-1] * fold_sign
    return jnp.concatenate([south_pad, zonal_ext, north_pad], axis=-2)


def reference(heat_centre_value, saltiness_centre, easting_transport_ratio, northing_transport_ratio, sinking_transport_ratio, spreading_number, seawater_indicator, bottom_water_layer):
    floor_depth = (seawater_indicator * bottom_water_layer).astype(jnp.float32)
    fields = (easting_transport_ratio, northing_transport_ratio, sinking_transport_ratio, spreading_number, floor_depth)
    fold_signs = (-1.0, -1.0, 1.0, 1.0, 1.0)
    grown = [extend_grid(field, 2, sign_value) for field, sign_value in zip(fields, fold_signs)]
    carried_quantities = jnp.stack([heat_centre_value, saltiness_centre])
    for step_index in range(2):
        carried_quantities = advance(extend_grid(carried_quantities, 2, 1.0), *grown)
    return carried_quantities[0], carried_quantities[1]
```

```python
import jax
import jax.numpy as jnp
from jax import lax
from jax.experimental import pallas as pl
from jax.experimental.pallas import tpu as pltpu
from jax.sharding import PartitionSpec as P

NK = 16
NJ = 16
NS = 8
NL = 128
F32 = jnp.float32
EAST, WEST = 0, 1
SOUTH, NORTH = 0, 1


def limiter(centred, a, b):
    upper = jnp.maximum(jnp.minimum(a, b), 0.0)
    lower = jnp.minimum(jnp.maximum(a, b), 0.0)
    return jnp.maximum(jnp.minimum(centred, upper), lower)


def quarter_edge(s):
    a = jnp.abs(s)
    return a * (0.25 - 0.25 * a)


def kernel(
    t_hbm, s_hbm, u_hbm, v_hbm, w_hbm, k_hbm, sea_hbm, bot_hbm,
    tout_hbm, sout_hbm,
    q0, q1, ob, ub, wb, vb, kb, seab, botb, flb,
    ox, sx, bx, ex, oy, sy, by, ey, oz, sz, ez,
    ax, dy, hy, fy,
    hq, hk, hv, hs, hb,
    pq, pr, uko, ukr, flo, flr, cc,
    eo, es, eb, ec, ed,
    in_sem, out_sem, row_send, row_recv, row2_send, row2_recv,
    col_send, col_recv, col2_send, col2_recv,
):
    ia = lax.axis_index("ia")
    ja = lax.axis_index("ja")
    n_ia = lax.axis_size("ia")
    n_ja = lax.axis_size("ja")
    top = ja == n_ja - 1
    low = ja > 0
    east = {"ia": lax.rem(ia + 1, n_ia), "ja": ja}
    west = {"ia": lax.rem(ia + n_ia - 1, n_ia), "ja": ja}
    north = {"ia": jnp.where(top, n_ia - 1 - ia, ia), "ja": jnp.where(top, ja, ja + 1)}
    south = {"ia": ia, "ja": jnp.maximum(ja - 1, 0)}
    nslot = jnp.where(top, NORTH, SOUTH)
    mesh_ids = pl.DeviceIdType.MESH

    lane = lax.broadcasted_iota(jnp.int32, (NS, NL), 1)
    sub = lax.broadcasted_iota(jnp.int32, (NS, NL), 0)
    l4 = lane & 3
    group = lane >> 2
    edge_lanes = ((lane + 2) & (NL - 1)) < 4

    barrier = pltpu.get_barrier_semaphore()
    for device in (east, west, north):
        pl.semaphore_signal(barrier, inc=1, device_id=device, device_id_type=mesh_ids)

    @pl.when(low)
    def _():
        pl.semaphore_signal(barrier, inc=1, device_id=south, device_id_type=mesh_ids)

    def load(index, src, dst3, lead):
        for s in range(NS):
            rows = pl.ds(NJ * s, NJ)
            if lead:
                pltpu.make_async_copy(src.at[:, rows, :], dst3(s), in_sem.at[index]).start()
            else:
                pltpu.make_async_copy(src.at[rows, :], dst3(s), in_sem.at[index]).start()

    load(0, t_hbm, lambda s: q0.at[0, :, pl.ds(2, NJ), s, :], True)
    load(1, s_hbm, lambda s: q0.at[1, :, pl.ds(2, NJ), s, :], True)
    load(2, sea_hbm, lambda s: seab.at[pl.ds(2, NJ), s, :], False)
    load(3, bot_hbm, lambda s: botb.at[pl.ds(2, NJ), s, :], False)
    load(4, u_hbm, lambda s: ub.at[:, :, s, :], True)
    load(5, k_hbm, lambda s: kb.at[:, pl.ds(1, NJ), s, :], True)
    load(6, v_hbm, lambda s: vb.at[:, pl.ds(1, NJ), s, :], True)
    load(7, w_hbm, lambda s: wb.at[:, :, s, :], True)

    def loaded(index, whole):
        pltpu.make_async_copy(whole, whole, in_sem.at[index]).wait()

    pl.semaphore_wait(barrier, jnp.where(low, 4, 3))

    def remote(src, dst, ssem, rsem, device):
        return pltpu.make_async_remote_copy(
            src_ref=src, dst_ref=dst, send_sem=ssem, recv_sem=rsem,
            device_id=device, device_id_type=mesh_ids,
        )

    def row_copies(first, last, slot, direction, device):
        pair = pl.ds(first, 2)
        line = pl.ds(last, 1)
        parts = [
            (t_hbm.at[:, pair, :], hq.at[0, slot, 0, :, :, 0, :]),
            (s_hbm.at[:, pair, :], hq.at[0, slot, 1, :, :, 0, :]),
            (k_hbm.at[:, line, :], hk.at[slot, :, :, 0, :]),
            (v_hbm.at[:, line, :], hv.at[slot, :, :, 0, :]),
            (sea_hbm.at[pair, :], hs.at[slot, :, 0, :]),
            (bot_hbm.at[pair, :], hb.at[slot, :, 0, :]),
        ]
        return [
            remote(src, dst, row_send.at[direction, n], row_recv.at[slot, n], device)
            for n, (src, dst) in enumerate(parts)
        ]

    rows_total = NJ * NS

    def north_rows(slot):
        return row_copies(rows_total - 2, rows_total - 1, slot, 0, north)

    def south_rows():
        return row_copies(0, 0, NORTH, 1, south)

    for copy in north_rows(nslot):
        copy.start()

    @pl.when(low)
    def _():
        for copy in south_rows():
            copy.start()

    def pack(load_vreg, count):
        acc = jnp.zeros((NS, NL), F32)
        for n in range(count):
            moved = pltpu.roll(load_vreg(n), (4 * n + 2) % NL, 1)
            acc = jnp.where(group == n, moved, acc)
        return acc

    def col_copies(step, part):
        first, size = ((2, 8), (10, 6), (0, 2))[part]
        sl = pl.ds(first, size)
        return [
            remote(pq.at[step, sl], pr.at[step, EAST, sl], col2_send.at[step, 0, part], col2_recv.at[step, EAST, part], west),
            remote(pq.at[step, sl], pr.at[step, WEST, sl], col2_send.at[step, 1, part], col2_recv.at[step, WEST, part], east),
        ]

    def static_col_copies():
        return [
            remote(uko, ukr.at[EAST], col_send.at[0, 0], col_recv.at[EAST, 0], west),
            remote(uko, ukr.at[WEST], col_send.at[1, 0], col_recv.at[WEST, 0], east),
            remote(flo, flr.at[EAST], col_send.at[0, 1], col_recv.at[EAST, 1], west),
            remote(flo, flr.at[WEST], col_send.at[1, 1], col_recv.at[WEST, 1], east),
        ]

    loaded(0, q0.at[0, :, pl.ds(2, NJ)])
    loaded(1, q0.at[1, :, pl.ds(2, NJ)])

    @pl.loop(0, NJ // 2)
    def _(half):
        for h in range(2):
            j = 2 * half + h
            pq[0, j] = pack(lambda n: q0[n // NK, n % NK, j + 2], 2 * NK)

    for part in range(3):
        for copy in col_copies(0, part):
            copy.start()

    loaded(2, seab.at[pl.ds(2, NJ)])
    loaded(3, botb.at[pl.ds(2, NJ)])
    for j in range(2, NJ + 2):
        flb[j] = (seab[j] * botb[j]).astype(F32)
    flo[...] = pack(lambda n: flb[n + 2], NJ)
    loaded(4, ub)
    loaded(5, kb.at[:, pl.ds(1, NJ)])

    @pl.loop(0, NJ // 2)
    def _(half):
        for h in range(2):
            j = 2 * half + h
            uko[j] = pack(lambda n: ub[n, j] if n < NK else kb[n - NK, j + 1], 2 * NK)

    for copy in static_col_copies():
        copy.start()

    loaded(6, vb.at[:, pl.ds(1, NJ)])
    loaded(7, wb)

    def open_y(j):
        face = jnp.minimum(flb[j + 2], flb[j + 3])
        for k in range(NK):
            oy[k, j + 2] = jnp.where(face > k, 4.0, 0.0)

    def coef_y(j):
        face = jnp.minimum(flb[j + 2], flb[j + 3])
        for k in range(NK):
            v = vb[k, j + 1]
            sy[k, j + 1] = jnp.where(face > k, v, 0.0)
            by[k, j + 1] = jnp.minimum(0.25 * v, 0.0) - 0.125 * (kb[k, j + 1] + kb[k, j + 2])
            ey[k, j + 1] = quarter_edge(v)

    @pl.loop(0, NJ)
    def _(j):
        fl = flb[j + 2]
        face = jnp.where(lane == NL - 1, 0.0, jnp.minimum(fl, pltpu.roll(fl, NL - 1, 1)))
        for k in range(NK):
            is_open = face > k
            u = ub[k, j]
            kap = kb[k, j + 1]
            ox[k, j] = jnp.where(is_open, 4.0, 0.0)
            sx[k, j] = jnp.where(is_open, u, 0.0)
            bx[k, j] = jnp.minimum(0.25 * u, 0.0) - 0.125 * (kap + pltpu.roll(kap, NL - 1, 1))
            ex[k, j] = quarter_edge(u)
            if k < NK - 1:
                below = fl > k + 1
                w = wb[k, j]
                oz[k, j] = jnp.where(below, 4.0, 0.0)
                sz[k, j] = jnp.where(below, w, 0.0)
                ez[k, j] = quarter_edge(w)

    @pl.loop(0, NJ - 1)
    def _(j):
        open_y(j)
        coef_y(j)

    south_sub = (sub == 0) & low
    north_sub = sub == 0

    def mirror(x):
        return jnp.take_along_axis(x, NL - 1 - lane, axis=1)

    def from_south(halo, own):
        return jnp.where(south_sub, halo, pltpu.roll(own, 1, 0))

    def from_north(halo, own):
        return pltpu.roll(jnp.where(north_sub, halo, own), NS - 1, 0)

    def fold_q(step):
        @pl.when(top)
        def _():
            for t in range(2):
                @pl.loop(0, NK // 4)
                def _(kk):
                    for k4 in range(4):
                        k = 4 * kk + k4
                        near = mirror(hq[step, NORTH, t, k, 1])
                        far = mirror(hq[step, NORTH, t, k, 0])
                        hq[step, NORTH, t, k, 0] = near
                        hq[step, NORTH, t, k, 1] = far

    def halo_q(step, q):
        fold_q(step)

        @pl.loop(0, NK // 4)
        def _(kk):
            for k4 in range(4):
                k = 4 * kk + k4
                for t in range(2):
                    for r in range(2):
                        q[t, k, r] = from_south(hq[step, SOUTH, t, k, r], q[t, k, NJ + r])
                        q[t, k, NJ + 2 + r] = from_north(hq[step, NORTH, t, k, r], q[t, k, 2 + r])

    def wait_rows(slot):
        for copy in (row_copies(0, 0, slot, 0, north)):
            copy.wait_recv()

    wait_rows(NORTH)

    @pl.when(low)
    def _():
        wait_rows(SOUTH)

    @pl.when(top)
    def _():
        for k in range(NK):
            hk[NORTH, k, 0] = mirror(hk[NORTH, k, 0])
        for h in (hs, hb):
            near = mirror(h[NORTH, 1])
            far = mirror(h[NORTH, 0])
            h[NORTH, 0] = near
            h[NORTH, 1] = far

    for r in range(2):
        south_floor = (hs[SOUTH, r] * hb[SOUTH, r]).astype(F32)
        north_floor = (hs[NORTH, r] * hb[NORTH, r]).astype(F32)
        flb[r] = jnp.where(
            sub == 0, jnp.where(low, south_floor, 0.0), pltpu.roll(flb[NJ + r], 1, 0)
        )
        flb[NJ + 2 + r] = from_north(north_floor, flb[2 + r])
    for k in range(NK):
        kb[k, 0] = from_south(hk[SOUTH, k, 0], kb[k, NJ])
        kb[k, NJ + 1] = from_north(hk[NORTH, k, 0], kb[k, 1])
        vb[k, 0] = from_south(hv[SOUTH, k, 0], vb[k, NJ])
    for j in (-2, -1, NJ - 1, NJ):
        open_y(j)
    for j in (-1, NJ - 1):
        coef_y(j)
    halo_q(0, q0)

    for copy in static_col_copies():
        copy.wait_recv()

    level4 = (group & (NK - 1)).astype(F32)

    @pl.loop(0, NJ // 4)
    def _(quarter):
        for j4 in range(4):
            j = 4 * quarter + j4
            index = 4 * j + l4

            def spread(x):
                return jnp.take_along_axis(x, index, axis=1)

            own_f, east_f, west_f = spread(flo[...]), spread(flr[EAST]), spread(flr[WEST])

            def halves(x):
                other = pltpu.roll(x, NL // 2, 1)
                return jnp.where(lane < NL // 2, x, other), jnp.where(lane < NL // 2, other, x)

            own_u, own_k = halves(uko[j])
            _, east_k = halves(ukr[EAST, j])
            west_u, west_k = halves(ukr[WEST, j])
            first = l4 < 2
            for side in (EAST, WEST):
                if side == EAST:
                    floor, u, kap = jnp.where(first, own_f, east_f), own_u, jnp.where(first, own_k, east_k)
                else:
                    floor, u, kap = (
                        jnp.where(first, west_f, own_f),
                        jnp.where(first, west_u, own_u),
                        jnp.where(first, west_k, own_k),
                    )
                face = jnp.minimum(floor, pltpu.roll(floor, NL - 1, 1))
                is_open = (face > level4) & (l4 < 3)
                b = jnp.minimum(0.25 * u, 0.0) - 0.125 * (kap + pltpu.roll(kap, NL - 1, 1))
                e = quarter_edge(u)
                outer = l4 == 1
                eo[side, j] = jnp.where(is_open, 4.0, 0.0)
                es[side, j] = jnp.where(is_open & outer, u, 0.0)
                eb[side, j] = jnp.where(outer, b, 0.0)
                if side == EAST:
                    c_lanes, d_lanes = outer, first
                else:
                    c_lanes, d_lanes = (l4 == 1) | (l4 == 2), outer
                ec[side, j] = jnp.where((u > 0) & c_lanes, e, 0.0)
                ed[side, j] = jnp.where((u <= 0) & d_lanes, e, 0.0)

    def edge_correction(step, j):
        own = pq[step, j]
        first = l4 < 2
        sums = []
        for side in (EAST, WEST):
            if side == EAST:
                win = jnp.where(first, own, pr[step, EAST, j])
            else:
                win = jnp.where(first, pr[step, WEST, j], own)
            d = (pltpu.roll(win, NL - 1, 1) - win) * eo[side, j]
            before = pltpu.roll(d, 1, 1)
            h = limiter(0.25 * (d + before), before, d)
            g = es[side, j] * win + eb[side, j] * d + ec[side, j] * h + ed[side, j] * pltpu.roll(h, NL - 1, 1)
            sums.append(pltpu.roll(g, 1, 1) - g)
        cc[j] = jnp.where(first, sums[EAST], sums[WEST])

    def edges(step, part):
        for copy in col_copies(step, part):
            copy.wait_recv()
        first, size = ((2, 8), (10, 6), (0, 2))[part]
        for j in range(first, first + size):
            edge_correction(step, j)

    def zonal(q, j):
        correction = cc[j]
        for k in range(NK):
            o, s, b, e = ox[k, j], sx[k, j], bx[k, j], ex[k, j]
            up = s > 0
            for t in range(2):
                x = q[t, k, j + 2]
                d = (pltpu.roll(x, NL - 1, 1) - x) * o
                before = pltpu.roll(d, 1, 1)
                h = limiter(0.25 * (d + before), before, d)
                f = s * x + b * d + e * jnp.where(up, h, pltpu.roll(h, NL - 1, 1))
                n = NK * t + k
                fix = jnp.where(edge_lanes, pltpu.roll(correction, (NL - 2 - 4 * n) % NL, 1), 0.0)
                ax[t, k] = pltpu.roll(f, 1, 1) - f + fix

    def meridional_start(q, j):
        @pl.loop(0, NK // 4)
        def _(kk):
            for k4 in range(4):
                k = 4 * kk + k4
                s, b, e = sy[k, j], by[k, j], ey[k, j]
                for t in range(2):
                    a2, a1, c0, c1 = (q[t, k, j + n] for n in range(4))
                    d2 = (a1 - a2) * oy[k, j]
                    d1 = (c0 - a1) * oy[k, j + 1]
                    d0 = (c1 - c0) * oy[k, j + 2]
                    h1 = limiter(c0 - a2, d2, d1)
                    h0 = limiter(c1 - a1, d1, d0)
                    dy[t, k] = d0
                    hy[t, k] = h0
                    fy[t, k] = s * a1 + b * d1 + e * jnp.where(s > 0, h1, h0)

    def rest(q, out, off, j, step):
        fl = flb[j + 2]
        packed = jnp.zeros((NS, NL), F32)
        state = []
        for t in range(2):
            x0, x1 = q[t, 0, j + 2], q[t, 1, j + 2]
            d0 = (x1 - x0) * oz[0, j]
            state.append([x0, x1, d0, None, None])
        for k in range(NK):
            s, b, e = sy[k, j + 1], by[k, j + 1], ey[k, j + 1]
            up = s > 0
            oy1 = oy[k, j + 3]
            if k < NK - 1:
                zs, ze = sz[k, j], ez[k, j]
                zup = zs > 0
            if k < NK - 2:
                zo = oz[k + 1, j]
            wet = fl > k
            for t in range(2):
                x, below, zd, zh, zf = state[t]
                y1, y2 = q[t, k, j + 3], q[t, k, j + 4]
                d0, h0 = dy[t, k], hy[t, k]
                d1 = (y2 - y1) * oy1
                h1 = limiter(y2 - x, d0, d1)
                f = s * x + b * d0 + e * jnp.where(up, h0, h1)
                acc = (ax[t, k] + fy[t, k]) - f
                dy[t, k] = d1
                hy[t, k] = h1
                fy[t, k] = f
                if k < NK - 1:
                    if k < NK - 2:
                        deeper = q[t, k + 2, j + 2]
                        zd1 = (deeper - below) * zo
                        zh1 = limiter(deeper - x, zd, zd1)
                    else:
                        deeper, zd1, zh1 = None, None, None
                    slope_near = 0.0 if zh is None else zh
                    slope_far = 0.0 if zh1 is None else zh1
                    nf = zs * jnp.where(zup, x, below) + ze * jnp.where(zup, slope_near, slope_far)
                    acc = acc - nf
                    state[t] = [below, deeper, zd1, zh1, nf]
                if zf is not None:
                    acc = acc + zf
                if step == 0:
                    new = jnp.where(wet, x, 0.0) + acc
                else:
                    new = x + acc
                out[t, k, j + off] = new
                if step == 0:
                    n = NK * t + k
                    moved = pltpu.roll(jnp.where(edge_lanes, new, 0.0), (4 * n + 2) % NL, 1)
                    packed = packed + moved
        if step == 0:
            pq[1, j] = packed

    def sweep(q, out, off, step, at_edge_b, at_rows, at_half):
        zonal(q, 2)
        meridional_start(q, 2)

        @pl.loop(0, NJ)
        def _(i):
            j = (i + 2) & (NJ - 1)

            @pl.when(i == 7)
            def _():
                at_edge_b()

            @pl.when(i == 8)
            def _():
                at_half()

            @pl.when(i == 12)
            def _():
                at_rows()

            @pl.when(i == 14)
            def _():
                meridional_start(q, 0)

            rest(q, out, off, j, step)
            zonal(q, (j + 1) & (NJ - 1))

    def nothing():
        pass

    def send_half():
        for copy in col_copies(1, 0):
            copy.start()

    for part in range(3):
        edges(0, part)
    sweep(q0, q1, 2, 0, nothing, nothing, send_half)
    for part in (1, 2):
        for copy in col_copies(1, part):
            copy.start()

    def row2_north(slot):
        return remote(
            q1.at[:, :, pl.ds(NJ, 2), NS - 1, :], hq.at[1, slot, :, :, :, 0, :],
            row2_send.at[0], row2_recv.at[slot], north,
        )

    def row2_south():
        return remote(
            q1.at[:, :, pl.ds(2, 2), 0, :], hq.at[1, NORTH, :, :, :, 0, :],
            row2_send.at[1], row2_recv.at[NORTH], south,
        )

    row2_north(nslot).start()

    @pl.when(low)
    def _():
        row2_south().start()

    def at_edge_b():
        edges(1, 1)
        edges(1, 2)

    def at_rows():
        row2_north(NORTH).wait_recv()

        @pl.when(low)
        def _():
            row2_north(SOUTH).wait_recv()

        halo_q(1, q1)

    def out_copies(part):
        first, size = ((2, 8), (10, 6), (0, 2))[part]
        return [
            pltpu.make_async_copy(
                ob.at[t, :, pl.ds(first, size), s, :],
                dst.at[:, pl.ds(NJ * s + first, size), :],
                out_sem.at[t, s, part],
            )
            for t, dst in enumerate((tout_hbm, sout_hbm))
            for s in range(NS)
        ]

    def out_half():
        for copy in out_copies(0):
            copy.start()

    edges(1, 0)
    sweep(q1, ob, 0, 1, at_edge_b, at_rows, out_half)
    for part in (1, 2):
        for copy in out_copies(part):
            copy.start()

    for copy in north_rows(nslot):
        copy.wait_send()
    row2_north(nslot).wait_send()

    @pl.when(low)
    def _():
        for copy in south_rows():
            copy.wait_send()
        row2_south().wait_send()

    for copy in static_col_copies():
        copy.wait_send()
    for step in range(2):
        for part in range(3):
            for copy in col_copies(step, part):
                copy.wait_send()
    for part in range(3):
        for copy in out_copies(part):
            copy.wait()


def on_device(t, s, u, v, w, kap, sea, bot):
    def vm(*lead):
        return pltpu.VMEM(lead + (NS, NL), F32)

    def vi(*lead):
        return pltpu.VMEM(lead + (NS, NL), jnp.int32)

    dma = pltpu.SemaphoreType.DMA
    anywhere = pl.BlockSpec(memory_space=pl.ANY)
    shape = jax.ShapeDtypeStruct(t.shape, F32)
    return pl.pallas_call(
        kernel,
        out_shape=(shape, shape),
        in_specs=[anywhere] * 8,
        out_specs=(anywhere, anywhere),
        scratch_shapes=[
            vm(2, NK, NJ + 4), vm(2, NK, NJ + 4), vm(2, NK, NJ),
            vm(NK, NJ), vm(NK, NJ), vm(NK, NJ + 1), vm(NK, NJ + 2),
            vi(NJ + 4), vi(NJ + 4), vm(NJ + 4),
            vm(NK, NJ), vm(NK, NJ), vm(NK, NJ), vm(NK, NJ),
            vm(NK, NJ + 3), vm(NK, NJ + 1), vm(NK, NJ + 1), vm(NK, NJ + 1),
            vm(NK, NJ), vm(NK, NJ), vm(NK, NJ),
            vm(2, NK), vm(2, NK), vm(2, NK), vm(2, NK),
            vm(2, 2, 2, NK, 2), vm(2, NK, 1), vm(2, NK, 1), vi(2, 2), vi(2, 2),
            vm(2, NJ), vm(2, 2, NJ), vm(NJ), vm(2, NJ), vm(), vm(2), vm(NJ),
            vm(2, NJ), vm(2, NJ), vm(2, NJ), vm(2, NJ), vm(2, NJ),
            dma((8,)), dma((2, NS, 3)), dma((2, 6)), dma((2, 6)), dma((2,)), dma((2,)),
            dma((2, 2)), dma((2, 2)), dma((2, 2, 3)), dma((2, 2, 3)),
        ],
        compiler_params=pltpu.CompilerParams(
            collective_id=0, has_side_effects=True, vmem_limit_bytes=50 * 1024 * 1024
        ),
        cost_estimate=pl.CostEstimate(flops=120_000_000, bytes_accessed=9_000_000, transcendentals=0),
    )(t, s, u, v, w, kap, sea, bot)


def solution(mesh):
    block = P(None, "ja", "ia")
    flat = P("ja", "ia")
    return jax.shard_map(
        on_device,
        mesh=mesh,
        in_specs=(block,) * 6 + (flat, flat),
        out_specs=(block, block),
        check_vma=False,
    )
```

```python
import jax
import jax.numpy as jnp
from jax import lax
from jax.experimental import pallas as pl
from jax.experimental.pallas import tpu as pltpu
from jax.sharding import PartitionSpec as P

NK = 16
NJ = 16
NS = 8
NL = 128
F32 = jnp.float32
EAST, WEST = 0, 1
SOUTH, NORTH = 0, 1


def limiter(centred, a, b):
    upper = jnp.maximum(jnp.minimum(a, b), 0.0)
    lower = jnp.minimum(jnp.maximum(a, b), 0.0)
    return jnp.maximum(jnp.minimum(centred, upper), lower)


def quarter_edge(s):
    a = jnp.abs(s)
    return a * (0.25 - 0.25 * a)


def kernel(
    t_hbm, s_hbm, u_hbm, v_hbm, w_hbm, k_hbm, sea_hbm, bot_hbm,
    tout_hbm, sout_hbm,
    q0, q1, ob, ub, wb, vb, kb, seab, botb, flb,
    ox, sx, bx, ex, oy, sy, by, ey, oz, sz, ez,
    oxw, dx, hx, fx, dy, hy, fy,
    hq, hk, hv, hs, hb,
    pq, pr, uko, ukr, flo, flr, cc,
    eo, es, eb, ec, ed,
    in_sem, out_sem, row_send, row_recv, row2_send, row2_recv,
    col_send, col_recv, col2_send, col2_recv,
):
    ia = lax.axis_index("ia")
    ja = lax.axis_index("ja")
    n_ia = lax.axis_size("ia")
    n_ja = lax.axis_size("ja")
    top = ja == n_ja - 1
    low = ja > 0
    east = {"ia": lax.rem(ia + 1, n_ia), "ja": ja}
    west = {"ia": lax.rem(ia + n_ia - 1, n_ia), "ja": ja}
    north = {"ia": jnp.where(top, n_ia - 1 - ia, ia), "ja": jnp.where(top, ja, ja + 1)}
    south = {"ia": ia, "ja": jnp.maximum(ja - 1, 0)}
    nslot = jnp.where(top, NORTH, SOUTH)
    mesh_ids = pl.DeviceIdType.MESH

    lane = lax.broadcasted_iota(jnp.int32, (NS, NL), 1)
    sub = lax.broadcasted_iota(jnp.int32, (NS, NL), 0)
    l4 = lane & 3
    group = lane >> 2
    edge_lanes = ((lane + 2) & (NL - 1)) < 4

    barrier = pltpu.get_barrier_semaphore()
    for device in (east, west, north):
        pl.semaphore_signal(barrier, inc=1, device_id=device, device_id_type=mesh_ids)

    @pl.when(low)
    def _():
        pl.semaphore_signal(barrier, inc=1, device_id=south, device_id_type=mesh_ids)

    def load(index, src, dst3, lead):
        for s in range(NS):
            rows = pl.ds(NJ * s, NJ)
            if lead:
                pltpu.make_async_copy(src.at[:, rows, :], dst3(s), in_sem.at[index]).start()
            else:
                pltpu.make_async_copy(src.at[rows, :], dst3(s), in_sem.at[index]).start()

    load(0, t_hbm, lambda s: q0.at[0, :, pl.ds(2, NJ), s, :], True)
    load(1, s_hbm, lambda s: q0.at[1, :, pl.ds(2, NJ), s, :], True)
    load(2, sea_hbm, lambda s: seab.at[pl.ds(2, NJ), s, :], False)
    load(3, bot_hbm, lambda s: botb.at[pl.ds(2, NJ), s, :], False)
    load(4, u_hbm, lambda s: ub.at[:, :, s, :], True)
    load(5, k_hbm, lambda s: kb.at[:, pl.ds(1, NJ), s, :], True)
    load(6, v_hbm, lambda s: vb.at[:, pl.ds(1, NJ), s, :], True)
    load(7, w_hbm, lambda s: wb.at[:, :, s, :], True)

    def loaded(index, whole):
        pltpu.make_async_copy(whole, whole, in_sem.at[index]).wait()

    pl.semaphore_wait(barrier, jnp.where(low, 4, 3))

    def remote(src, dst, ssem, rsem, device):
        return pltpu.make_async_remote_copy(
            src_ref=src, dst_ref=dst, send_sem=ssem, recv_sem=rsem,
            device_id=device, device_id_type=mesh_ids,
        )

    def row_copies(first, last, slot, direction, device):
        pair = pl.ds(first, 2)
        line = pl.ds(last, 1)
        parts = [
            (t_hbm.at[:, pair, :], hq.at[0, slot, 0, :, :, 0, :]),
            (s_hbm.at[:, pair, :], hq.at[0, slot, 1, :, :, 0, :]),
            (k_hbm.at[:, line, :], hk.at[slot, :, :, 0, :]),
            (v_hbm.at[:, line, :], hv.at[slot, :, :, 0, :]),
            (sea_hbm.at[pair, :], hs.at[slot, :, 0, :]),
            (bot_hbm.at[pair, :], hb.at[slot, :, 0, :]),
        ]
        return [
            remote(src, dst, row_send.at[direction, n], row_recv.at[slot, n], device)
            for n, (src, dst) in enumerate(parts)
        ]

    rows_total = NJ * NS

    def north_rows(slot):
        return row_copies(rows_total - 2, rows_total - 1, slot, 0, north)

    def south_rows():
        return row_copies(0, 0, NORTH, 1, south)

    for copy in north_rows(nslot):
        copy.start()

    @pl.when(low)
    def _():
        for copy in south_rows():
            copy.start()

    def pack(load_vreg, count):
        acc = jnp.zeros((NS, NL), F32)
        for n in range(count):
            moved = pltpu.roll(load_vreg(n), (4 * n + 2) % NL, 1)
            acc = jnp.where(group == n, moved, acc)
        return acc

    def col_copies(step, part):
        first, size = ((2, 8), (10, 6), (0, 2))[part]
        sl = pl.ds(first, size)
        return [
            remote(pq.at[step, sl], pr.at[step, EAST, sl], col2_send.at[step, 0, part], col2_recv.at[step, EAST, part], west),
            remote(pq.at[step, sl], pr.at[step, WEST, sl], col2_send.at[step, 1, part], col2_recv.at[step, WEST, part], east),
        ]

    def static_col_copies():
        return [
            remote(uko, ukr.at[EAST], col_send.at[0, 0], col_recv.at[EAST, 0], west),
            remote(uko, ukr.at[WEST], col_send.at[1, 0], col_recv.at[WEST, 0], east),
            remote(flo, flr.at[EAST], col_send.at[0, 1], col_recv.at[EAST, 1], west),
            remote(flo, flr.at[WEST], col_send.at[1, 1], col_recv.at[WEST, 1], east),
        ]

    loaded(0, q0.at[0, :, pl.ds(2, NJ)])
    loaded(1, q0.at[1, :, pl.ds(2, NJ)])

    @pl.loop(0, NJ // 2)
    def _(half):
        for h in range(2):
            j = 2 * half + h
            pq[0, j] = pack(lambda n: q0[n // NK, n % NK, j + 2], 2 * NK)

    for part in range(3):
        for copy in col_copies(0, part):
            copy.start()

    loaded(2, seab.at[pl.ds(2, NJ)])
    loaded(3, botb.at[pl.ds(2, NJ)])
    for j in range(2, NJ + 2):
        flb[j] = (seab[j] * botb[j]).astype(F32)
    flo[...] = pack(lambda n: flb[n + 2], NJ)
    loaded(4, ub)
    loaded(5, kb.at[:, pl.ds(1, NJ)])

    @pl.loop(0, NJ // 2)
    def _(half):
        for h in range(2):
            j = 2 * half + h
            uko[j] = pack(lambda n: ub[n, j] if n < NK else kb[n - NK, j + 1], 2 * NK)

    for copy in static_col_copies():
        copy.start()

    loaded(6, vb.at[:, pl.ds(1, NJ)])
    loaded(7, wb)

    def open_y(j):
        face = jnp.minimum(flb[j + 2], flb[j + 3])
        for k in range(NK):
            oy[k, j + 2] = jnp.where(face > k, 4.0, 0.0)

    def coef_y(j):
        face = jnp.minimum(flb[j + 2], flb[j + 3])
        for k in range(NK):
            v = vb[k, j + 1]
            sy[k, j + 1] = jnp.where(face > k, v, 0.0)
            by[k, j + 1] = jnp.minimum(0.25 * v, 0.0) - 0.125 * (kb[k, j + 1] + kb[k, j + 2])
            ey[k, j + 1] = quarter_edge(v)

    @pl.loop(0, NJ)
    def _(j):
        fl = flb[j + 2]
        face = jnp.where(lane == NL - 1, 0.0, jnp.minimum(fl, pltpu.roll(fl, NL - 1, 1)))
        face_w = jnp.where(lane == 0, 0.0, jnp.minimum(fl, pltpu.roll(fl, 1, 1)))
        for k in range(NK):
            is_open = face > k
            u = ub[k, j]
            kap = kb[k, j + 1]
            ox[k, j] = jnp.where(is_open, 4.0, 0.0)
            oxw[k, j] = jnp.where(face_w > k, 4.0, 0.0)
            sx[k, j] = jnp.where(is_open, u, 0.0)
            bx[k, j] = jnp.minimum(0.25 * u, 0.0) - 0.125 * (kap + pltpu.roll(kap, NL - 1, 1))
            ex[k, j] = quarter_edge(u)
            if k < NK - 1:
                below = fl > k + 1
                w = wb[k, j]
                oz[k, j] = jnp.where(below, 4.0, 0.0)
                sz[k, j] = jnp.where(below, w, 0.0)
                ez[k, j] = quarter_edge(w)

    @pl.loop(0, NJ - 1)
    def _(j):
        open_y(j)
        coef_y(j)

    south_sub = (sub == 0) & low
    north_sub = sub == 0

    def mirror(x):
        return jnp.take_along_axis(x, NL - 1 - lane, axis=1)

    def from_south(halo, own):
        return jnp.where(south_sub, halo, pltpu.roll(own, 1, 0))

    def from_north(halo, own):
        return pltpu.roll(jnp.where(north_sub, halo, own), NS - 1, 0)

    def fold_q(step):
        @pl.when(top)
        def _():
            for t in range(2):
                for k in range(NK):
                    near = mirror(hq[step, NORTH, t, k, 1])
                    far = mirror(hq[step, NORTH, t, k, 0])
                    hq[step, NORTH, t, k, 0] = near
                    hq[step, NORTH, t, k, 1] = far

    def halo_q(step, q):
        fold_q(step)

        @pl.loop(0, NK // 4)
        def _(kk):
            for k4 in range(4):
                k = 4 * kk + k4
                for t in range(2):
                    for r in range(2):
                        q[t, k, r] = from_south(hq[step, SOUTH, t, k, r], q[t, k, NJ + r])
                        q[t, k, NJ + 2 + r] = from_north(hq[step, NORTH, t, k, r], q[t, k, 2 + r])

    def wait_rows(slot):
        for copy in (row_copies(0, 0, slot, 0, north)):
            copy.wait_recv()

    wait_rows(NORTH)

    @pl.when(low)
    def _():
        wait_rows(SOUTH)

    @pl.when(top)
    def _():
        for k in range(NK):
            hk[NORTH, k, 0] = mirror(hk[NORTH, k, 0])
        for h in (hs, hb):
            near = mirror(h[NORTH, 1])
            far = mirror(h[NORTH, 0])
            h[NORTH, 0] = near
            h[NORTH, 1] = far

    for r in range(2):
        south_floor = (hs[SOUTH, r] * hb[SOUTH, r]).astype(F32)
        north_floor = (hs[NORTH, r] * hb[NORTH, r]).astype(F32)
        flb[r] = jnp.where(
            sub == 0, jnp.where(low, south_floor, 0.0), pltpu.roll(flb[NJ + r], 1, 0)
        )
        flb[NJ + 2 + r] = from_north(north_floor, flb[2 + r])
    for k in range(NK):
        kb[k, 0] = from_south(hk[SOUTH, k, 0], kb[k, NJ])
        kb[k, NJ + 1] = from_north(hk[NORTH, k, 0], kb[k, 1])
        vb[k, 0] = from_south(hv[SOUTH, k, 0], vb[k, NJ])
    for j in (-2, -1, NJ - 1, NJ):
        open_y(j)
    for j in (-1, NJ - 1):
        coef_y(j)
    halo_q(0, q0)

    for copy in static_col_copies():
        copy.wait_recv()

    level4 = (group & (NK - 1)).astype(F32)

    @pl.loop(0, NJ // 4)
    def _(quarter):
        for j4 in range(4):
            j = 4 * quarter + j4
            index = 4 * j + l4

            def spread(x):
                return jnp.take_along_axis(x, index, axis=1)

            own_f, east_f, west_f = spread(flo[...]), spread(flr[EAST]), spread(flr[WEST])

            def halves(x):
                other = pltpu.roll(x, NL // 2, 1)
                return jnp.where(lane < NL // 2, x, other), jnp.where(lane < NL // 2, other, x)

            own_u, own_k = halves(uko[j])
            _, east_k = halves(ukr[EAST, j])
            west_u, west_k = halves(ukr[WEST, j])
            first = l4 < 2
            for side in (EAST, WEST):
                if side == EAST:
                    floor, u, kap = jnp.where(first, own_f, east_f), own_u, jnp.where(first, own_k, east_k)
                else:
                    floor, u, kap = (
                        jnp.where(first, west_f, own_f),
                        jnp.where(first, west_u, own_u),
                        jnp.where(first, west_k, own_k),
                    )
                face = jnp.minimum(floor, pltpu.roll(floor, NL - 1, 1))
                is_open = (face > level4) & (l4 < 3)
                b = jnp.minimum(0.25 * u, 0.0) - 0.125 * (kap + pltpu.roll(kap, NL - 1, 1))
                e = quarter_edge(u)
                outer = l4 == 1
                eo[side, j] = jnp.where(is_open, 4.0, 0.0)
                es[side, j] = jnp.where(is_open & outer, u, 0.0)
                eb[side, j] = jnp.where(outer, b, 0.0)
                if side == EAST:
                    c_lanes, d_lanes = outer, first
                else:
                    c_lanes, d_lanes = (l4 == 1) | (l4 == 2), outer
                ec[side, j] = jnp.where((u > 0) & c_lanes, e, 0.0)
                ed[side, j] = jnp.where((u <= 0) & d_lanes, e, 0.0)

    def edge_correction(step, j):
        own = pq[step, j]
        first = l4 < 2
        sums = []
        for side in (EAST, WEST):
            if side == EAST:
                win = jnp.where(first, own, pr[step, EAST, j])
            else:
                win = jnp.where(first, pr[step, WEST, j], own)
            d = (pltpu.roll(win, NL - 1, 1) - win) * eo[side, j]
            before = pltpu.roll(d, 1, 1)
            h = limiter(0.25 * (d + before), before, d)
            g = es[side, j] * win + eb[side, j] * d + ec[side, j] * h + ed[side, j] * pltpu.roll(h, NL - 1, 1)
            sums.append(pltpu.roll(g, 1, 1) - g)
        cc[j] = jnp.where(first, sums[EAST], sums[WEST])

    def edges(step, part):
        for copy in col_copies(step, part):
            copy.wait_recv()
        first, size = ((2, 8), (10, 6), (0, 2))[part]
        for j in range(first, first + size):
            edge_correction(step, j)

    def zonal_slopes(q, j, slot):
        for k in range(NK):
            o, ow = ox[k, j], oxw[k, j]
            for t in range(2):
                x = q[t, k, j + 2]
                after = pltpu.roll(x, NL - 1, 1)
                before = pltpu.roll(x, 1, 1)
                d = (after - x) * o
                dx[slot, t, k] = d
                hx[slot, t, k] = limiter(after - before, (x - before) * ow, d)

    def zonal_fluxes(q, j, slot):
        for k in range(NK):
            s, b, e = sx[k, j], bx[k, j], ex[k, j]
            up = s > 0
            for t in range(2):
                x, d, h = q[t, k, j + 2], dx[slot, t, k], hx[slot, t, k]
                fx[slot, t, k] = s * x + b * d + e * jnp.where(up, h, pltpu.roll(h, NL - 1, 1))

    def repack(out, off, j):
        sums = []
        for t in range(2):
            for k in range(NK):
                n = NK * t + k
                moved = pltpu.roll(jnp.where(edge_lanes, out[t, k, j + off], 0.0), (4 * n + 2) % NL, 1)
                if len(sums) < 4:
                    sums.append(moved)
                else:
                    sums[n % 4] = sums[n % 4] + moved
        pq[1, j] = (sums[0] + sums[1]) + (sums[2] + sums[3])

    def meridional_start(q, j):
        @pl.loop(0, NK // 4)
        def _(kk):
            for k4 in range(4):
                k = 4 * kk + k4
                s, b, e = sy[k, j], by[k, j], ey[k, j]
                for t in range(2):
                    a2, a1, c0, c1 = (q[t, k, j + n] for n in range(4))
                    d2 = (a1 - a2) * oy[k, j]
                    d1 = (c0 - a1) * oy[k, j + 1]
                    d0 = (c1 - c0) * oy[k, j + 2]
                    h1 = limiter(c0 - a2, d2, d1)
                    h0 = limiter(c1 - a1, d1, d0)
                    dy[t, k] = d0
                    hy[t, k] = h0
                    fy[t, k] = s * a1 + b * d1 + e * jnp.where(s > 0, h1, h0)

    def rest(q, out, off, j, step, slot):
        fl = flb[j + 2]
        correction = cc[j]
        state = []
        for t in range(2):
            x0, x1 = q[t, 0, j + 2], q[t, 1, j + 2]
            d0 = (x1 - x0) * oz[0, j]
            state.append([x0, x1, d0, None, None])
        for k in range(NK):
            s, b, e = sy[k, j + 1], by[k, j + 1], ey[k, j + 1]
            up = s > 0
            oy1 = oy[k, j + 3]
            if k < NK - 1:
                zs, ze = sz[k, j], ez[k, j]
                zup = zs > 0
            if k < NK - 2:
                zo = oz[k + 1, j]
            wet = fl > k
            for t in range(2):
                x, below, zd, zh, zf = state[t]
                y1, y2 = q[t, k, j + 3], q[t, k, j + 4]
                d0, h0 = dy[t, k], hy[t, k]
                d1 = (y2 - y1) * oy1
                h1 = limiter(y2 - x, d0, d1)
                f = s * x + b * d0 + e * jnp.where(up, h0, h1)
                n = NK * t + k
                flux = fx[slot, t, k]
                fix = jnp.where(edge_lanes, pltpu.roll(correction, (NL - 2 - 4 * n) % NL, 1), 0.0)
                acc = ((pltpu.roll(flux, 1, 1) - flux) + (fy[t, k] - f)) + fix
                dy[t, k] = d1
                hy[t, k] = h1
                fy[t, k] = f
                if k < NK - 1:
                    if k < NK - 2:
                        deeper = q[t, k + 2, j + 2]
                        zd1 = (deeper - below) * zo
                        zh1 = limiter(deeper - x, zd, zd1)
                    else:
                        deeper, zd1, zh1 = None, None, None
                    slope_near = 0.0 if zh is None else zh
                    slope_far = 0.0 if zh1 is None else zh1
                    nf = zs * jnp.where(zup, x, below) + ze * jnp.where(zup, slope_near, slope_far)
                    acc = acc - nf
                    state[t] = [below, deeper, zd1, zh1, nf]
                if zf is not None:
                    acc = acc + zf
                if step == 0:
                    new = jnp.where(wet, x, 0.0) + acc
                else:
                    new = x + acc
                out[t, k, j + off] = new

    def sweep(q, out, off, step, at_edge_b, at_rows, at_half):
        zonal_slopes(q, 2, 0)
        zonal_slopes(q, 3, 1)
        zonal_fluxes(q, 2, 0)
        meridional_start(q, 2)

        @pl.loop(0, NJ // 2)
        def _(i):
            @pl.when(i == 4)
            def _():
                at_edge_b()

            @pl.when(i == 5)
            def _():
                at_half()

            @pl.when(i == 6)
            def _():
                at_rows()

            @pl.when(i == 7)
            def _():
                meridional_start(q, 0)

            for half in range(2):
                j = (2 * i + 2 + half) & (NJ - 1)
                if step == 0:
                    repack(out, off, (j - 1) & (NJ - 1))
                rest(q, out, off, j, step, half)
                zonal_fluxes(q, (j + 1) & (NJ - 1), 1 - half)
                zonal_slopes(q, (j + 2) & (NJ - 1), half)

        if step == 0:
            repack(out, off, 1)

    def nothing():
        pass

    def send_half():
        for copy in col_copies(1, 0):
            copy.start()

    for part in range(3):
        edges(0, part)
    sweep(q0, q1, 2, 0, nothing, nothing, send_half)
    for part in (1, 2):
        for copy in col_copies(1, part):
            copy.start()

    def row2_north(slot):
        return remote(
            q1.at[:, :, pl.ds(NJ, 2), NS - 1, :], hq.at[1, slot, :, :, :, 0, :],
            row2_send.at[0], row2_recv.at[slot], north,
        )

    def row2_south():
        return remote(
            q1.at[:, :, pl.ds(2, 2), 0, :], hq.at[1, NORTH, :, :, :, 0, :],
            row2_send.at[1], row2_recv.at[NORTH], south,
        )

    row2_north(nslot).start()

    @pl.when(low)
    def _():
        row2_south().start()

    def at_edge_b():
        edges(1, 1)
        edges(1, 2)

    def at_rows():
        row2_north(NORTH).wait_recv()

        @pl.when(low)
        def _():
            row2_north(SOUTH).wait_recv()

        halo_q(1, q1)

    def out_copies(part):
        first, size = ((2, 8), (10, 6), (0, 2))[part]
        return [
            pltpu.make_async_copy(
                ob.at[t, :, pl.ds(first, size), s, :],
                dst.at[:, pl.ds(NJ * s + first, size), :],
                out_sem.at[t, s, part],
            )
            for t, dst in enumerate((tout_hbm, sout_hbm))
            for s in range(NS)
        ]

    def out_half():
        for copy in out_copies(0):
            copy.start()

    edges(1, 0)
    sweep(q1, ob, 0, 1, at_edge_b, at_rows, out_half)
    for part in (1, 2):
        for copy in out_copies(part):
            copy.start()

    for copy in north_rows(nslot):
        copy.wait_send()
    row2_north(nslot).wait_send()

    @pl.when(low)
    def _():
        for copy in south_rows():
            copy.wait_send()
        row2_south().wait_send()

    for copy in static_col_copies():
        copy.wait_send()
    for step in range(2):
        for part in range(3):
            for copy in col_copies(step, part):
                copy.wait_send()
    for part in range(3):
        for copy in out_copies(part):
            copy.wait()


def on_device(t, s, u, v, w, kap, sea, bot):
    def vm(*lead):
        return pltpu.VMEM(lead + (NS, NL), F32)

    def vi(*lead):
        return pltpu.VMEM(lead + (NS, NL), jnp.int32)

    dma = pltpu.SemaphoreType.DMA
    anywhere = pl.BlockSpec(memory_space=pl.ANY)
    shape = jax.ShapeDtypeStruct(t.shape, F32)
    return pl.pallas_call(
        kernel,
        out_shape=(shape, shape),
        in_specs=[anywhere] * 8,
        out_specs=(anywhere, anywhere),
        scratch_shapes=[
            vm(2, NK, NJ + 4), vm(2, NK, NJ + 4), vm(2, NK, NJ),
            vm(NK, NJ), vm(NK, NJ), vm(NK, NJ + 1), vm(NK, NJ + 2),
            vi(NJ + 4), vi(NJ + 4), vm(NJ + 4),
            vm(NK, NJ), vm(NK, NJ), vm(NK, NJ), vm(NK, NJ),
            vm(NK, NJ + 3), vm(NK, NJ + 1), vm(NK, NJ + 1), vm(NK, NJ + 1),
            vm(NK, NJ), vm(NK, NJ), vm(NK, NJ),
            vm(NK, NJ), vm(2, 2, NK), vm(2, 2, NK), vm(2, 2, NK), vm(2, NK), vm(2, NK), vm(2, NK),
            vm(2, 2, 2, NK, 2), vm(2, NK, 1), vm(2, NK, 1), vi(2, 2), vi(2, 2),
            vm(2, NJ), vm(2, 2, NJ), vm(NJ), vm(2, NJ), vm(), vm(2), vm(NJ),
            vm(2, NJ), vm(2, NJ), vm(2, NJ), vm(2, NJ), vm(2, NJ),
            dma((8,)), dma((2, NS, 3)), dma((2, 6)), dma((2, 6)), dma((2,)), dma((2,)),
            dma((2, 2)), dma((2, 2)), dma((2, 2, 3)), dma((2, 2, 3)),
        ],
        compiler_params=pltpu.CompilerParams(
            collective_id=0, has_side_effects=True, vmem_limit_bytes=58 * 1024 * 1024
        ),
        cost_estimate=pl.CostEstimate(flops=120_000_000, bytes_accessed=9_000_000, transcendentals=0),
    )(t, s, u, v, w, kap, sea, bot)


def solution(mesh):
    block = P(None, "ja", "ia")
    flat = P("ja", "ia")
    return jax.shard_map(
        on_device,
        mesh=mesh,
        in_specs=(block,) * 6 + (flat, flat),
        out_specs=(block, block),
        check_vma=False,
    )
```

```python
import jax
import jax.numpy as jnp
from jax import lax
from jax.experimental import pallas as pl
from jax.experimental.pallas import tpu as pltpu
from jax.sharding import PartitionSpec as P

NK = 16
NJ = 16
NS = 8
NL = 128
F32 = jnp.float32
EAST, WEST = 0, 1
SOUTH, NORTH = 0, 1


def limiter(centred, a, b):
    upper = jnp.maximum(jnp.minimum(a, b), 0.0)
    lower = jnp.minimum(jnp.maximum(a, b), 0.0)
    return jnp.maximum(jnp.minimum(centred, upper), lower)


def quarter_edge(s):
    a = jnp.abs(s)
    return a * (0.25 - 0.25 * a)


def kernel(
    t_hbm, s_hbm, u_hbm, v_hbm, w_hbm, k_hbm, sea_hbm, bot_hbm,
    tout_hbm, sout_hbm,
    q0, q1, ob, ub, wb, vb, kb, seab, botb, flb,
    ox, sx, bx, ex, oy, sy, by, ey, oz, sz, ez,
    oxw, dx, hx, fx, dy, hy, fy,
    rown, rhal, rk, rkh, rv, rvh, hs, hb, rcoef, rc,
    pq, pr, uko, ukr, flo, flr, cc,
    eo, es, eb, ec, ed,
    in_sem, own_sem, own2_sem, out_sem, row_send, row_recv, row2_send, row2_recv,
    col_send, col_recv, col2_send, col2_recv,
):
    ia = lax.axis_index("ia")
    ja = lax.axis_index("ja")
    n_ia = lax.axis_size("ia")
    n_ja = lax.axis_size("ja")
    top = ja == n_ja - 1
    low = ja > 0
    east = {"ia": lax.rem(ia + 1, n_ia), "ja": ja}
    west = {"ia": lax.rem(ia + n_ia - 1, n_ia), "ja": ja}
    north = {"ia": jnp.where(top, n_ia - 1 - ia, ia), "ja": jnp.where(top, ja, ja + 1)}
    south = {"ia": ia, "ja": jnp.maximum(ja - 1, 0)}
    nslot = jnp.where(top, NORTH, SOUTH)
    mesh_ids = pl.DeviceIdType.MESH

    lane = lax.broadcasted_iota(jnp.int32, (NS, NL), 1)
    sub = lax.broadcasted_iota(jnp.int32, (NS, NL), 0)
    l4 = lane & 3
    group = lane >> 2
    edge_lanes = ((lane + 2) & (NL - 1)) < 4

    barrier = pltpu.get_barrier_semaphore()
    for device in (east, west, north):
        pl.semaphore_signal(barrier, inc=1, device_id=device, device_id_type=mesh_ids)

    @pl.when(low)
    def _():
        pl.semaphore_signal(barrier, inc=1, device_id=south, device_id_type=mesh_ids)

    def load(index, src, dst3, lead):
        for s in range(NS):
            rows = pl.ds(NJ * s, NJ)
            if lead:
                pltpu.make_async_copy(src.at[:, rows, :], dst3(s), in_sem.at[index]).start()
            else:
                pltpu.make_async_copy(src.at[rows, :], dst3(s), in_sem.at[index]).start()

    load(0, t_hbm, lambda s: q0.at[0, :, pl.ds(2, NJ), s, :], True)
    load(1, s_hbm, lambda s: q0.at[1, :, pl.ds(2, NJ), s, :], True)
    load(2, sea_hbm, lambda s: seab.at[pl.ds(2, NJ), s, :], False)
    load(3, bot_hbm, lambda s: botb.at[pl.ds(2, NJ), s, :], False)
    load(4, u_hbm, lambda s: ub.at[:, :, s, :], True)
    load(5, k_hbm, lambda s: kb.at[:, pl.ds(1, NJ), s, :], True)
    load(6, v_hbm, lambda s: vb.at[:, pl.ds(1, NJ), s, :], True)
    load(7, w_hbm, lambda s: wb.at[:, :, s, :], True)

    def loaded(index, whole):
        pltpu.make_async_copy(whole, whole, in_sem.at[index]).wait()

    rows_total = NJ * NS
    edge_rows = (0, 1, rows_total - 2, rows_total - 1)

    def own_row_copies():
        pairs = [
            (src.at[:, row, :], rown.at[0, t, a])
            for t, src in enumerate((t_hbm, s_hbm))
            for a, row in enumerate(edge_rows)
        ]
        pairs += [(k_hbm.at[:, row, :], rk.at[a]) for a, row in enumerate((0, rows_total - 1))]
        pairs += [(v_hbm.at[:, row, :], rv.at[a]) for a, row in enumerate((0, rows_total - 2, rows_total - 1))]
        return [pltpu.make_async_copy(a, b, own_sem.at[n]) for n, (a, b) in enumerate(pairs)]

    for copy in own_row_copies():
        copy.start()

    def remote(src, dst, ssem, rsem, device):
        return pltpu.make_async_remote_copy(
            src_ref=src, dst_ref=dst, send_sem=ssem, recv_sem=rsem,
            device_id=device, device_id_type=mesh_ids,
        )

    def row_copies(first, last, slot, direction, device):
        pair = pl.ds(first, 2)
        parts = [
            (src.at[:, first + r, :], rhal.at[0, slot, t, r])
            for t, src in enumerate((t_hbm, s_hbm))
            for r in range(2)
        ] + [
            (k_hbm.at[:, last, :], rkh.at[slot]),
            (v_hbm.at[:, last, :], rvh.at[slot]),
            (sea_hbm.at[pair, :], hs.at[slot]),
            (bot_hbm.at[pair, :], hb.at[slot]),
        ]
        return [
            remote(src, dst, row_send.at[direction, n], row_recv.at[slot, n], device)
            for n, (src, dst) in enumerate(parts)
        ]

    def north_rows(slot):
        return row_copies(rows_total - 2, rows_total - 1, slot, 0, north)

    def south_rows():
        return row_copies(0, 0, NORTH, 1, south)

    def pack(load_vreg, count):
        acc = jnp.zeros((NS, NL), F32)
        for n in range(count):
            moved = pltpu.roll(load_vreg(n), (4 * n + 2) % NL, 1)
            acc = jnp.where(group == n, moved, acc)
        return acc

    PARTS = ((0, NJ),), ((2, NJ - 4), (NJ - 2, 2), (0, 2))

    def col_copies(step, part):
        first, size = PARTS[step][part]
        sl = pl.ds(first, size)
        return [
            remote(pq.at[step, sl], pr.at[step, EAST, sl], col2_send.at[step, 0, part], col2_recv.at[step, EAST, part], west),
            remote(pq.at[step, sl], pr.at[step, WEST, sl], col2_send.at[step, 1, part], col2_recv.at[step, WEST, part], east),
        ]

    def static_col_copies():
        return [
            remote(uko, ukr.at[EAST], col_send.at[0, 0], col_recv.at[EAST, 0], west),
            remote(uko, ukr.at[WEST], col_send.at[1, 0], col_recv.at[WEST, 0], east),
            remote(flo, flr.at[EAST], col_send.at[0, 1], col_recv.at[EAST, 1], west),
            remote(flo, flr.at[WEST], col_send.at[1, 1], col_recv.at[WEST, 1], east),
        ]

    loaded(0, q0.at[0, :, pl.ds(2, NJ)])
    loaded(1, q0.at[1, :, pl.ds(2, NJ)])

    @pl.loop(0, NJ // 4)
    def _(quarter):
        for h in range(4):
            j = 4 * quarter + h
            pq[0, j] = pack(lambda n: q0[n // NK, n % NK, j + 2], 2 * NK)

    loaded(2, seab.at[pl.ds(2, NJ)])
    loaded(3, botb.at[pl.ds(2, NJ)])
    for j in range(2, NJ + 2):
        flb[j] = (seab[j] * botb[j]).astype(F32)
    flo[...] = pack(lambda n: flb[n + 2], NJ)
    loaded(4, ub)
    loaded(5, kb.at[:, pl.ds(1, NJ)])

    @pl.loop(0, NJ // 4)
    def _(quarter):
        for h in range(4):
            j = 4 * quarter + h
            uko[j] = pack(lambda n: ub[n, j] if n < NK else kb[n - NK, j + 1], 2 * NK)

    def first_sends():
        pl.semaphore_wait(barrier, jnp.where(low, 4, 3))
        for copy in col_copies(0, 0):
            copy.start()
        for copy in north_rows(nslot):
            copy.start()

        @pl.when(low)
        def _():
            for copy in south_rows():
                copy.start()

        for copy in static_col_copies():
            copy.start()

    loaded(6, vb.at[:, pl.ds(1, NJ)])
    loaded(7, wb)

    def open_y(j):
        face = jnp.minimum(flb[j + 2], flb[j + 3])
        for k in range(NK):
            oy[k, j + 2] = jnp.where(face > k, 4.0, 0.0)

    def coef_y(j):
        face = jnp.minimum(flb[j + 2], flb[j + 3])
        for k in range(NK):
            v = vb[k, j + 1]
            sy[k, j + 1] = jnp.where(face > k, v, 0.0)
            by[k, j + 1] = jnp.minimum(0.25 * v, 0.0) - 0.125 * (kb[k, j + 1] + kb[k, j + 2])
            ey[k, j + 1] = quarter_edge(v)

    @pl.loop(0, NJ)
    def _(j):
        fl = flb[j + 2]
        face = jnp.where(lane == NL - 1, 0.0, jnp.minimum(fl, pltpu.roll(fl, NL - 1, 1)))
        face_w = jnp.where(lane == 0, 0.0, jnp.minimum(fl, pltpu.roll(fl, 1, 1)))
        for k in range(NK):
            is_open = face > k
            u = ub[k, j]
            kap = kb[k, j + 1]
            ox[k, j] = jnp.where(is_open, 4.0, 0.0)
            oxw[k, j] = jnp.where(face_w > k, 4.0, 0.0)
            sx[k, j] = jnp.where(is_open, u, 0.0)
            bx[k, j] = jnp.minimum(0.25 * u, 0.0) - 0.125 * (kap + pltpu.roll(kap, NL - 1, 1))
            ex[k, j] = quarter_edge(u)
            if k < NK - 1:
                below = fl > k + 1
                w = wb[k, j]
                oz[k, j] = jnp.where(below, 4.0, 0.0)
                sz[k, j] = jnp.where(below, w, 0.0)
                ez[k, j] = quarter_edge(w)

    @pl.loop(0, NJ - 1)
    def _(j):
        open_y(j)
        coef_y(j)

    for r in range(2):
        flb[r] = jnp.where(sub == 0, 0.0, pltpu.roll(flb[NJ + r], 1, 0))
        flb[NJ + 2 + r] = jnp.where(sub == NS - 1, 0.0, pltpu.roll(flb[2 + r], NS - 1, 0))
    for k in range(NK):
        kb[k, 0] = pltpu.roll(kb[k, NJ], 1, 0)
        kb[k, NJ + 1] = pltpu.roll(kb[k, 1], NS - 1, 0)
        vb[k, 0] = pltpu.roll(vb[k, NJ], 1, 0)
    for j in (-2, -1, NJ - 1, NJ):
        open_y(j)
    for j in (-1, NJ - 1):
        coef_y(j)

    def wrap_rows(q):
        for t in range(2):
            for k in range(NK):
                for r in range(2):
                    q[t, k, r] = pltpu.roll(q[t, k, NJ + r], 1, 0)
                    q[t, k, NJ + 2 + r] = pltpu.roll(q[t, k, 2 + r], NS - 1, 0)

    wrap_rows(q0)
    first_sends()

    def mirror(x):
        return jnp.take_along_axis(x, NL - 1 - lane, axis=1)

    def levels(kk):
        return pl.ds(NS * kk, NS)

    def fold(step):
        @pl.when(top)
        def _():
            for t in range(2):
                for kk in range(NK // NS):
                    lv = levels(kk)
                    near = mirror(rhal[step, NORTH, t, 1, lv, :])
                    far = mirror(rhal[step, NORTH, t, 0, lv, :])
                    rhal[step, NORTH, t, 0, lv, :] = near
                    rhal[step, NORTH, t, 1, lv, :] = far
            if step == 0:
                for kk in range(NK // NS):
                    rkh[NORTH, levels(kk), :] = mirror(rkh[NORTH, levels(kk), :])
                for h in (hs, hb):
                    near = mirror(jnp.broadcast_to(h[NORTH, 1:2, :], (NS, NL)))
                    far = mirror(jnp.broadcast_to(h[NORTH, 0:1, :], (NS, NL)))
                    h[NORTH, 0:1, :] = near[0:1]
                    h[NORTH, 1:2, :] = far[0:1]

    def row_static():
        def line(x):
            return jnp.broadcast_to(x, (NS, NL))

        def halo_floor(slot, r):
            return line((hs[slot, r : r + 1, :] * hb[slot, r : r + 1, :]).astype(F32))

        south_floors = [
            jnp.where(low, halo_floor(SOUTH, 0), 0.0),
            jnp.where(low, halo_floor(SOUTH, 1), 0.0),
            line(flb[2, 0:1, :]),
            line(flb[3, 0:1, :]),
        ]
        north_floors = [
            line(flb[NJ, NS - 1 : NS, :]),
            line(flb[NJ + 1, NS - 1 : NS, :]),
            halo_floor(NORTH, 0),
            halo_floor(NORTH, 1),
        ]
        for kk in range(NK // NS):
            lv = levels(kk)
            depth = (sub + NS * kk).astype(F32)
            for side, floors in ((SOUTH, south_floors), (NORTH, north_floors)):
                if side == SOUTH:
                    v = jnp.where(low, rvh[SOUTH, lv, :], 0.0)
                    ka, kc = jnp.where(low, rkh[SOUTH, lv, :], 0.0), rk[0, lv, :]
                    inner = rv[0, lv, :]
                    keep = inner > 0
                else:
                    v = rv[2, lv, :]
                    ka, kc = rk[1, lv, :], rkh[NORTH, lv, :]
                    inner = rv[1, lv, :]
                    keep = inner <= 0
                for n in range(3):
                    is_open = jnp.minimum(floors[n], floors[n + 1]) > depth
                    rcoef[side, n, lv, :] = jnp.where(is_open, 4.0, 0.0)
                    if n == 1:
                        rcoef[side, 3, lv, :] = jnp.where(is_open, v, 0.0)
                rcoef[side, 4, lv, :] = jnp.minimum(0.25 * v, 0.0) - 0.125 * (ka + kc)
                rcoef[side, 5, lv, :] = quarter_edge(v)
                rcoef[side, 6, lv, :] = jnp.where(keep, quarter_edge(inner), 0.0)

    def row_correction(step):
        for t in range(2):
            for kk in range(NK // NS):
                lv = levels(kk)
                for side in (SOUTH, NORTH):
                    own = [rown[step, t, 2 * side + r, lv, :] for r in range(2)]
                    if side == SOUTH:
                        halo = [jnp.where(low, rhal[step, SOUTH, t, r, lv, :], 0.0) for r in range(2)]
                        w = halo + own
                    else:
                        halo = [rhal[step, NORTH, t, r, lv, :] for r in range(2)]
                        w = own + halo
                    d = [(w[n + 1] - w[n]) * rcoef[side, n, lv, :] for n in range(3)]
                    h1 = limiter(w[2] - w[0], d[0], d[1])
                    h2 = limiter(w[3] - w[1], d[1], d[2])
                    s = rcoef[side, 3, lv, :]
                    f = s * w[1] + rcoef[side, 4, lv, :] * d[1] + rcoef[side, 5, lv, :] * jnp.where(s > 0, h1, h2)
                    g = rcoef[side, 6, lv, :] * (h2 if side == SOUTH else h1)
                    if side == SOUTH:
                        rc[t, 0, lv, :] = f - g
                        rc[t, 1, lv, :] = g
                    else:
                        rc[t, 2, lv, :] = -g
                        rc[t, 3, lv, :] = g - f

    def add_rows(out, off):
        for a, (j, s) in enumerate(((0, 0), (1, 0), (NJ - 2, NS - 1), (NJ - 1, NS - 1))):
            for t in range(2):
                for k in range(NK):
                    out[t, k, j + off, s : s + 1, :] = out[t, k, j + off, s : s + 1, :] + rc[t, a, k : k + 1, :]

    def wait_rows(slot):
        for copy in row_copies(0, 0, slot, 0, north):
            copy.wait_recv()

    level4 = (group & (NK - 1)).astype(F32)

    def edge_static():
        for j in range(NJ):
            index = 4 * j + l4

            def spread(x):
                return jnp.take_along_axis(x, index, axis=1)

            own_f, east_f, west_f = spread(flo[...]), spread(flr[EAST]), spread(flr[WEST])

            def halves(x):
                other = pltpu.roll(x, NL // 2, 1)
                return jnp.where(lane < NL // 2, x, other), jnp.where(lane < NL // 2, other, x)

            own_u, own_k = halves(uko[j])
            _, east_k = halves(ukr[EAST, j])
            west_u, west_k = halves(ukr[WEST, j])
            first = l4 < 2
            for side in (EAST, WEST):
                if side == EAST:
                    floor, u, kap = jnp.where(first, own_f, east_f), own_u, jnp.where(first, own_k, east_k)
                else:
                    floor, u, kap = (
                        jnp.where(first, west_f, own_f),
                        jnp.where(first, west_u, own_u),
                        jnp.where(first, west_k, own_k),
                    )
                face = jnp.minimum(floor, pltpu.roll(floor, NL - 1, 1))
                is_open = (face > level4) & (l4 < 3)
                b = jnp.minimum(0.25 * u, 0.0) - 0.125 * (kap + pltpu.roll(kap, NL - 1, 1))
                e = quarter_edge(u)
                outer = l4 == 1
                eo[side, j] = jnp.where(is_open, 4.0, 0.0)
                es[side, j] = jnp.where(is_open & outer, u, 0.0)
                eb[side, j] = jnp.where(outer, b, 0.0)
                if side == EAST:
                    c_lanes, d_lanes = outer, first
                else:
                    c_lanes, d_lanes = (l4 == 1) | (l4 == 2), outer
                ec[side, j] = jnp.where((u > 0) & c_lanes, e, 0.0)
                ed[side, j] = jnp.where((u <= 0) & d_lanes, e, 0.0)

    def edge_correction(step, j):
        own = pq[step, j]
        first = l4 < 2
        sums = []
        for side in (EAST, WEST):
            if side == EAST:
                win = jnp.where(first, own, pr[step, EAST, j])
            else:
                win = jnp.where(first, pr[step, WEST, j], own)
            d = (pltpu.roll(win, NL - 1, 1) - win) * eo[side, j]
            before = pltpu.roll(d, 1, 1)
            h = limiter(0.25 * (d + before), before, d)
            g = es[side, j] * win + eb[side, j] * d + ec[side, j] * h + ed[side, j] * pltpu.roll(h, NL - 1, 1)
            sums.append(pltpu.roll(g, 1, 1) - g)
        cc[j] = jnp.where(first, sums[EAST], sums[WEST])

    def unpacked(j, n):
        return jnp.where(edge_lanes, pltpu.roll(cc[j], (NL - 2 - 4 * n) % NL, 1), 0.0)

    def add_columns(out, off, j):
        for t in range(2):
            for k in range(NK):
                out[t, k, j + off] = out[t, k, j + off] + unpacked(j, NK * t + k)

    def zonal_slopes(q, j, slot):
        for k in range(NK):
            o, ow = ox[k, j], oxw[k, j]
            for t in range(2):
                x = q[t, k, j + 2]
                after = pltpu.roll(x, NL - 1, 1)
                before = pltpu.roll(x, 1, 1)
                d = (after - x) * o
                dx[slot, t, k] = d
                hx[slot, t, k] = limiter(after - before, (x - before) * ow, d)

    def zonal_fluxes(q, j, slot):
        for k in range(NK):
            s, b, e = sx[k, j], bx[k, j], ex[k, j]
            up = s > 0
            for t in range(2):
                x, d, h = q[t, k, j + 2], dx[slot, t, k], hx[slot, t, k]
                fx[slot, t, k] = s * x + b * d + e * jnp.where(up, h, pltpu.roll(h, NL - 1, 1))

    def repack(out, off, j):
        sums = []
        for t in range(2):
            for k in range(NK):
                n = NK * t + k
                moved = pltpu.roll(jnp.where(edge_lanes, out[t, k, j + off], 0.0), (4 * n + 2) % NL, 1)
                if len(sums) < 4:
                    sums.append(moved)
                else:
                    sums[n % 4] = sums[n % 4] + moved
        pq[1, j] = (sums[0] + sums[1]) + (sums[2] + sums[3])

    def meridional_start(q, j):
        @pl.loop(0, NK // 4)
        def _(kk):
            for k4 in range(4):
                k = 4 * kk + k4
                s, b, e = sy[k, j], by[k, j], ey[k, j]
                for t in range(2):
                    a2, a1, c0, c1 = (q[t, k, j + n] for n in range(4))
                    d2 = (a1 - a2) * oy[k, j]
                    d1 = (c0 - a1) * oy[k, j + 1]
                    d0 = (c1 - c0) * oy[k, j + 2]
                    h1 = limiter(c0 - a2, d2, d1)
                    h0 = limiter(c1 - a1, d1, d0)
                    dy[t, k] = d0
                    hy[t, k] = h0
                    fy[t, k] = s * a1 + b * d1 + e * jnp.where(s > 0, h1, h0)

    def rest(q, out, off, j, step, slot, fix):
        fl = flb[j + 2]
        state = []
        for t in range(2):
            x0, x1 = q[t, 0, j + 2], q[t, 1, j + 2]
            d0 = (x1 - x0) * oz[0, j]
            state.append([x0, x1, d0, None, None])
        for k in range(NK):
            s, b, e = sy[k, j + 1], by[k, j + 1], ey[k, j + 1]
            up = s > 0
            oy1 = oy[k, j + 3]
            if k < NK - 1:
                zs, ze = sz[k, j], ez[k, j]
                zup = zs > 0
            if k < NK - 2:
                zo = oz[k + 1, j]
            wet = fl > k
            for t in range(2):
                x, below, zd, zh, zf = state[t]
                y1, y2 = q[t, k, j + 3], q[t, k, j + 4]
                d0, h0 = dy[t, k], hy[t, k]
                d1 = (y2 - y1) * oy1
                h1 = limiter(y2 - x, d0, d1)
                f = s * x + b * d0 + e * jnp.where(up, h0, h1)
                flux = fx[slot, t, k]
                acc = (pltpu.roll(flux, 1, 1) - flux) + (fy[t, k] - f)
                if fix:
                    acc = acc + unpacked(j, NK * t + k)
                dy[t, k] = d1
                hy[t, k] = h1
                fy[t, k] = f
                if k < NK - 1:
                    if k < NK - 2:
                        deeper = q[t, k + 2, j + 2]
                        zd1 = (deeper - below) * zo
                        zh1 = limiter(deeper - x, zd, zd1)
                    else:
                        deeper, zd1, zh1 = None, None, None
                    slope_near = 0.0 if zh is None else zh
                    slope_far = 0.0 if zh1 is None else zh1
                    nf = zs * jnp.where(zup, x, below) + ze * jnp.where(zup, slope_near, slope_far)
                    acc = acc - nf
                    state[t] = [below, deeper, zd1, zh1, nf]
                if zf is not None:
                    acc = acc + zf
                if step == 0:
                    new = jnp.where(wet, x, 0.0) + acc
                else:
                    new = x + acc
                out[t, k, j + off] = new

    def sweep(q, out, off, step, first, last, repacking, fixing_in, fixing_out, at_start):
        @pl.loop(first, last)
        def _(i):
            at_start(i)

            for half in range(2):
                j = (2 * i + 2 + half) & (NJ - 1)
                if repacking:
                    repack(out, off, (j - 1) & (NJ - 1))
                rest(q, out, off, j, step, half, fixing_out)
                zonal_fluxes(q, (j + 1) & (NJ - 1), 1 - half)
                zonal_slopes(q, (j + 2) & (NJ - 1), half)
                if fixing_in:
                    add_columns(q, 2, j + 3)
                if fixing_out:
                    add_columns(out, off, (j - NJ // 2) & (NJ - 1))

    def start_sweep(q):
        zonal_slopes(q, 2, 0)
        zonal_slopes(q, 3, 1)
        zonal_fluxes(q, 2, 0)
        meridional_start(q, 2)

    def restart(q):
        def at(i):
            @pl.when(i == 7)
            def _():
                meridional_start(q, 0)

        return at

    outer = (NJ - 2, NJ - 1, 0, 1)
    start_sweep(q0)
    sweep(q0, q1, 2, 0, 0, 8, True, False, False, restart(q0))

    for copy in own_row_copies():
        copy.wait()
    wait_rows(NORTH)

    @pl.when(low)
    def _():
        wait_rows(SOUTH)

    fold(0)
    row_static()
    row_correction(0)
    for copy in static_col_copies():
        copy.wait_recv()
    for copy in col_copies(0, 0):
        copy.wait_recv()
    edge_static()
    for j in range(NJ):
        edge_correction(0, j)
    for j in range(2, NJ - 2):
        pq[1, j] = pq[1, j] + cc[j]
    for copy in col_copies(1, 0):
        copy.start()
    add_rows(q1, 2)
    for j in outer:
        add_columns(q1, 2, j)

    def row2_copies(j, s, slot, direction, device):
        return [
            remote(
                q1.at[t, :, j + r + 2, s, :], rhal.at[1, slot, t, r],
                row2_send.at[direction, t, r], row2_recv.at[slot, t, r], device,
            )
            for t in range(2)
            for r in range(2)
        ]

    def north2(slot):
        return row2_copies(NJ - 2, NS - 1, slot, 0, north)

    def south2():
        return row2_copies(0, 0, NORTH, 1, south)

    def own2_copies():
        return [
            pltpu.make_async_copy(q1.at[t, :, j + 2, s, :], rown.at[1, t, a], own2_sem.at[t, a])
            for t in range(2)
            for a, (j, s) in enumerate(((0, 0), (1, 0), (NJ - 2, NS - 1), (NJ - 1, NS - 1)))
        ]

    for copy in north2(nslot):
        copy.start()

    @pl.when(low)
    def _():
        for copy in south2():
            copy.start()

    for copy in own2_copies():
        copy.start()
    for j in outer:
        repack(q1, 2, j)
    for part in (1, 2):
        for copy in col_copies(1, part):
            copy.start()

    for j in (2, 3, 4, NJ - 3):
        add_columns(q1, 2, j)
    wrap_rows(q1)
    start_sweep(q1)
    sweep(q1, ob, 0, 1, 0, 4, False, True, False, lambda i: None)

    for copy in own2_copies():
        copy.wait()
    for copy in north2(NORTH):
        copy.wait_recv()

    @pl.when(low)
    def _():
        for copy in north2(SOUTH):
            copy.wait_recv()

    fold(1)
    row_correction(1)
    for part in range(3):
        for copy in col_copies(1, part):
            copy.wait_recv()
    for j in range(NJ):
        edge_correction(1, j)

    OUTS = (2, 4), (10, 4), (6, 4), (14, 2), (0, 2)

    def out_copies(part):
        first, size = OUTS[part]
        return [
            pltpu.make_async_copy(
                ob.at[t, :, pl.ds(first, size), s, :],
                dst.at[:, pl.ds(NJ * s + first, size), :],
                out_sem.at[t, s, part],
            )
            for t, dst in enumerate((tout_hbm, sout_hbm))
            for s in range(NS)
        ]

    def at_start(i):
        @pl.when(i == 6)
        def _():
            for part in range(2):
                for copy in out_copies(part):
                    copy.start()

        restart(q1)(i)

    sweep(q1, ob, 0, 1, 4, 8, False, False, True, at_start)
    for copy in out_copies(2):
        copy.start()
    add_rows(ob, 0)
    for part in (3, 4):
        for copy in out_copies(part):
            copy.start()

    for copy in north_rows(nslot) + north2(nslot):
        copy.wait_send()

    @pl.when(low)
    def _():
        for copy in south_rows() + south2():
            copy.wait_send()

    for copy in static_col_copies():
        copy.wait_send()
    for step in range(2):
        for part in range(len(PARTS[step])):
            for copy in col_copies(step, part):
                copy.wait_send()
    for part in range(len(OUTS)):
        for copy in out_copies(part):
            copy.wait()


def on_device(t, s, u, v, w, kap, sea, bot):
    def vm(*lead):
        return pltpu.VMEM(lead + (NS, NL), F32)

    def rows(*lead):
        return pltpu.VMEM(lead + (NK, NL), F32)

    def vi(*lead):
        return pltpu.VMEM(lead + (NS, NL), jnp.int32)

    dma = pltpu.SemaphoreType.DMA
    anywhere = pl.BlockSpec(memory_space=pl.ANY)
    shape = jax.ShapeDtypeStruct(t.shape, F32)
    return pl.pallas_call(
        kernel,
        out_shape=(shape, shape),
        in_specs=[anywhere] * 8,
        out_specs=(anywhere, anywhere),
        scratch_shapes=[
            vm(2, NK, NJ + 4), vm(2, NK, NJ + 4), vm(2, NK, NJ),
            vm(NK, NJ), vm(NK, NJ), vm(NK, NJ + 1), vm(NK, NJ + 2),
            vi(NJ + 4), vi(NJ + 4), vm(NJ + 4),
            vm(NK, NJ), vm(NK, NJ), vm(NK, NJ), vm(NK, NJ),
            vm(NK, NJ + 3), vm(NK, NJ + 1), vm(NK, NJ + 1), vm(NK, NJ + 1),
            vm(NK, NJ), vm(NK, NJ), vm(NK, NJ),
            vm(NK, NJ), vm(2, 2, NK), vm(2, 2, NK), vm(2, 2, NK), vm(2, NK), vm(2, NK), vm(2, NK),
            rows(2, 2, 4), rows(2, 2, 2, 2), rows(2), rows(2), rows(3), rows(2),
            pltpu.VMEM((2, 2, NL), jnp.int32), pltpu.VMEM((2, 2, NL), jnp.int32), rows(2, 7), rows(2, 4),
            vm(2, NJ), vm(2, 2, NJ), vm(NJ), vm(2, NJ), vm(), vm(2), vm(NJ),
            vm(2, NJ), vm(2, NJ), vm(2, NJ), vm(2, NJ), vm(2, NJ),
            dma((8,)), dma((13,)), dma((2, 4)), dma((2, NS, 5)), dma((2, 8)), dma((2, 8)), dma((2, 2, 2)), dma((2, 2, 2)),
            dma((2, 2)), dma((2, 2)), dma((2, 2, 3)), dma((2, 2, 3)),
        ],
        compiler_params=pltpu.CompilerParams(
            collective_id=0, has_side_effects=True, vmem_limit_bytes=58 * 1024 * 1024
        ),
        cost_estimate=pl.CostEstimate(flops=120_000_000, bytes_accessed=9_000_000, transcendentals=0),
    )(t, s, u, v, w, kap, sea, bot)


def solution(mesh):
    block = P(None, "ja", "ia")
    flat = P("ja", "ia")
    return jax.shard_map(
        on_device,
        mesh=mesh,
        in_specs=(block,) * 6 + (flat, flat),
        out_specs=(block, block),
        check_vma=False,
    )
```

```python
import jax
import jax.numpy as jnp
from jax import lax
from jax.experimental import pallas as pl
from jax.experimental.pallas import tpu as pltpu
from jax.sharding import PartitionSpec as P

NK = 16
NJ = 16
NS = 8
NL = 128
F32 = jnp.float32
EAST, WEST = 0, 1
SOUTH, NORTH = 0, 1


def limiter(centred, a, b):
    upper = jnp.maximum(jnp.minimum(a, b), 0.0)
    lower = jnp.minimum(jnp.maximum(a, b), 0.0)
    return jnp.maximum(jnp.minimum(centred, upper), lower)


def quarter_edge(s):
    a = jnp.abs(s)
    return a * (0.25 - 0.25 * a)


def kernel(
    t_hbm, s_hbm, u_hbm, v_hbm, w_hbm, k_hbm, sea_hbm, bot_hbm,
    tout_hbm, sout_hbm,
    q0, q1, ob, ub, wb, vb, kb, seab, botb, flb,
    ox, sx, bx, ex, oy, sy, by, ey, oz, sz, ez,
    oxw, dx, hx, fx, dy, hy, fy,
    rown, rhal, rk, rkh, rv, rvh, hs, hb, rcoef, rc,
    pq, pr, sent, uko, sent_uk, got_uk, sent_k, got_k, flo, flr, cc,
    eo, es, eb, ec, ed,
    in_sem, own_sem, own2_sem, out_sem, row_send, row_recv, row2_send, row2_recv,
    col_send, col_recv, col2_send, col2_recv,
):
    ia = lax.axis_index("ia")
    ja = lax.axis_index("ja")
    n_ia = lax.axis_size("ia")
    n_ja = lax.axis_size("ja")
    top = ja == n_ja - 1
    low = ja > 0
    east = {"ia": lax.rem(ia + 1, n_ia), "ja": ja}
    west = {"ia": lax.rem(ia + n_ia - 1, n_ia), "ja": ja}
    north = {"ia": jnp.where(top, n_ia - 1 - ia, ia), "ja": jnp.where(top, ja, ja + 1)}
    south = {"ia": ia, "ja": jnp.maximum(ja - 1, 0)}
    nslot = jnp.where(top, NORTH, SOUTH)
    mesh_ids = pl.DeviceIdType.MESH

    lane = lax.broadcasted_iota(jnp.int32, (NS, NL), 1)
    sub = lax.broadcasted_iota(jnp.int32, (NS, NL), 0)
    l4 = lane & 3
    group = lane >> 2
    edge_lanes = ((lane + 2) & (NL - 1)) < 4

    barrier = pltpu.get_barrier_semaphore()
    for device in (east, west, north):
        pl.semaphore_signal(barrier, inc=1, device_id=device, device_id_type=mesh_ids)

    @pl.when(low)
    def _():
        pl.semaphore_signal(barrier, inc=1, device_id=south, device_id_type=mesh_ids)

    @pl.loop(0, NS)
    def _(s):
        rows = pl.ds(pl.multiple_of(NJ * s, NJ), NJ)
        inner = pl.ds(2, NJ)
        inner1 = pl.ds(1, NJ)
        for index, (src, dst) in enumerate((
            (t_hbm.at[:, rows, :], q0.at[0, :, inner, s, :]),
            (s_hbm.at[:, rows, :], q0.at[1, :, inner, s, :]),
            (sea_hbm.at[rows, :], seab.at[inner, s, :]),
            (bot_hbm.at[rows, :], botb.at[inner, s, :]),
            (u_hbm.at[:, rows, :], ub.at[:, :, s, :]),
            (k_hbm.at[:, rows, :], kb.at[:, inner1, s, :]),
            (v_hbm.at[:, rows, :], vb.at[:, inner1, s, :]),
            (w_hbm.at[:, rows, :], wb.at[:, :, s, :]),
        )):
            pltpu.make_async_copy(src, dst, in_sem.at[index]).start()

    def loaded(index, whole):
        pltpu.make_async_copy(whole, whole, in_sem.at[index]).wait()

    rows_total = NJ * NS
    edge_rows = (0, 1, rows_total - 2, rows_total - 1)

    def own_row_copies():
        pairs = [
            (src.at[:, row, :], rown.at[0, t, a])
            for t, src in enumerate((t_hbm, s_hbm))
            for a, row in enumerate(edge_rows)
        ]
        pairs += [(k_hbm.at[:, row, :], rk.at[a]) for a, row in enumerate((0, rows_total - 1))]
        pairs += [(v_hbm.at[:, row, :], rv.at[a]) for a, row in enumerate((0, rows_total - 2, rows_total - 1))]
        return [pltpu.make_async_copy(a, b, own_sem.at[n]) for n, (a, b) in enumerate(pairs)]

    for copy in own_row_copies():
        copy.start()

    def remote(src, dst, ssem, rsem, device):
        return pltpu.make_async_remote_copy(
            src_ref=src, dst_ref=dst, send_sem=ssem, recv_sem=rsem,
            device_id=device, device_id_type=mesh_ids,
        )

    def row_copies(first, last, slot, direction, device):
        pair = pl.ds(first, 2)
        parts = [
            (src.at[:, first + r, :], rhal.at[0, slot, t, r])
            for t, src in enumerate((t_hbm, s_hbm))
            for r in range(2)
        ] + [
            (k_hbm.at[:, last, :], rkh.at[slot]),
            (v_hbm.at[:, last, :], rvh.at[slot]),
            (sea_hbm.at[pair, :], hs.at[slot]),
            (bot_hbm.at[pair, :], hb.at[slot]),
        ]
        return [
            remote(src, dst, row_send.at[direction, n], row_recv.at[slot, n], device)
            for n, (src, dst) in enumerate(parts)
        ]

    def north_rows(slot):
        return row_copies(rows_total - 2, rows_total - 1, slot, 0, north)

    def south_rows():
        return row_copies(0, 0, NORTH, 1, south)

    def pack(load_vreg, count):
        acc = jnp.zeros((NS, NL), F32)
        for n in range(count):
            moved = pltpu.roll(load_vreg(n), (4 * n + 2) % NL, 1)
            acc = jnp.where(group == n, moved, acc)
        return acc

    PARTS = ((0, NJ // 2),), ((2, NJ // 2 - 4), (NJ // 2 - 2, 2), (0, 2))

    def squeeze(step, rows):
        pair = lane & 63
        index = 4 * (pair >> 1) + (pair & 1)
        first = lane < NL // 2
        for a in rows:
            for side in (EAST, WEST):
                at = index + (2 if side == WEST else 0)
                sent[step, side, a] = jnp.where(
                    first,
                    jnp.take_along_axis(pq[step, a], at, axis=1),
                    jnp.take_along_axis(pq[step, a + NJ // 2], at, axis=1),
                )

    def col_copies(step, part):
        first, size = PARTS[step][part]
        sl = pl.ds(first, size)
        return [
            remote(sent.at[step, WEST, sl], pr.at[step, EAST, sl], col2_send.at[step, 0, part], col2_recv.at[step, EAST, part], west),
            remote(sent.at[step, EAST, sl], pr.at[step, WEST, sl], col2_send.at[step, 1, part], col2_recv.at[step, WEST, part], east),
        ]

    def squeeze_static():
        quarter = lane & 31
        to_east = 4 * quarter + 1
        to_west = NL // 2 + 4 * (lane & 15) + 2
        for m in range(4):
            acc = jnp.take_along_axis(uko[m], to_east, axis=1)
            for n in range(1, 4):
                acc = jnp.where((lane >> 5) == n, jnp.take_along_axis(uko[m + 4 * n], to_east, axis=1), acc)
            sent_uk[m] = acc
        for m in range(2):
            acc = jnp.take_along_axis(uko[m], to_west, axis=1)
            for n in range(1, 8):
                acc = jnp.where((lane >> 4) == n, jnp.take_along_axis(uko[m + 2 * n], to_west, axis=1), acc)
            sent_k[m] = acc

    def static_col_copies():
        return [
            remote(sent_k, got_k, col_send.at[0, 0], col_recv.at[EAST, 0], west),
            remote(sent_uk, got_uk, col_send.at[1, 0], col_recv.at[WEST, 0], east),
            remote(flo, flr.at[EAST], col_send.at[0, 1], col_recv.at[EAST, 1], west),
            remote(flo, flr.at[WEST], col_send.at[1, 1], col_recv.at[WEST, 1], east),
        ]

    loaded(0, q0.at[0, :, pl.ds(2, NJ)])
    loaded(1, q0.at[1, :, pl.ds(2, NJ)])

    @pl.loop(0, NJ // 2)
    def _(half):
        for h in range(2):
            j = 2 * half + h
            pq[0, j] = pack(lambda n: q0[n // NK, n % NK, j + 2], 2 * NK)

    loaded(2, seab.at[pl.ds(2, NJ)])
    loaded(3, botb.at[pl.ds(2, NJ)])
    for j in range(2, NJ + 2):
        flb[j] = (seab[j] * botb[j]).astype(F32)
    flo[...] = pack(lambda n: flb[n + 2], NJ)
    loaded(4, ub)
    loaded(5, kb.at[:, pl.ds(1, NJ)])

    def first_sends():
        pl.semaphore_wait(barrier, jnp.where(low, 4, 3))
        for copy in col_copies(0, 0):
            copy.start()
        for copy in north_rows(nslot):
            copy.start()

        @pl.when(low)
        def _():
            for copy in south_rows():
                copy.start()

        for copy in static_col_copies():
            copy.start()

    loaded(6, vb.at[:, pl.ds(1, NJ)])
    loaded(7, wb)

    def open_y(j):
        face = jnp.minimum(flb[j + 2], flb[j + 3])
        for k in range(NK):
            oy[k, j + 2] = jnp.where(face > k, 4.0, 0.0)

    def coef_y(j):
        face = jnp.minimum(flb[j + 2], flb[j + 3])
        for k in range(NK):
            v = vb[k, j + 1]
            sy[k, j + 1] = jnp.where(face > k, v, 0.0)
            by[k, j + 1] = jnp.minimum(0.25 * v, 0.0) - 0.125 * (kb[k, j + 1] + kb[k, j + 2])
            ey[k, j + 1] = quarter_edge(v)

    @pl.loop(0, NJ)
    def _(j):
        fl = flb[j + 2]
        face = jnp.where(lane == NL - 1, 0.0, jnp.minimum(fl, pltpu.roll(fl, NL - 1, 1)))
        uko[j] = pack(lambda n: ub[n, j] if n < NK else kb[n - NK, j + 1], 2 * NK)
        face_w = jnp.where(lane == 0, 0.0, jnp.minimum(fl, pltpu.roll(fl, 1, 1)))
        for k in range(NK):
            is_open = face > k
            u = ub[k, j]
            kap = kb[k, j + 1]
            ox[k, j] = jnp.where(is_open, 4.0, 0.0)
            oxw[k, j] = jnp.where(face_w > k, 4.0, 0.0)
            sx[k, j] = jnp.where(is_open, u, 0.0)
            bx[k, j] = jnp.minimum(0.25 * u, 0.0) - 0.125 * (kap + pltpu.roll(kap, NL - 1, 1))
            ex[k, j] = quarter_edge(u)
            if k < NK - 1:
                below = fl > k + 1
                w = wb[k, j]
                oz[k, j] = jnp.where(below, 4.0, 0.0)
                sz[k, j] = jnp.where(below, w, 0.0)
                ez[k, j] = quarter_edge(w)

    for r in range(2):
        flb[r] = jnp.where(sub == 0, 0.0, pltpu.roll(flb[NJ + r], 1, 0))
        flb[NJ + 2 + r] = jnp.where(sub == NS - 1, 0.0, pltpu.roll(flb[2 + r], NS - 1, 0))
    for k in range(NK):
        kb[k, 0] = pltpu.roll(kb[k, NJ], 1, 0)
        kb[k, NJ + 1] = pltpu.roll(kb[k, 1], NS - 1, 0)
        vb[k, 0] = pltpu.roll(vb[k, NJ], 1, 0)

    @pl.loop(0, NJ + 1)
    def _(j):
        open_y(j - 1)
        coef_y(j - 1)

    @pl.loop(0, 2)
    def _(r):
        open_y((NJ + 2) * r - 2)

    def wrap_rows(q):
        @pl.loop(0, NK // 4)
        def _(kk):
            for k4 in range(4):
                k = 4 * kk + k4
                for t in range(2):
                    for r in range(2):
                        q[t, k, r] = pltpu.roll(q[t, k, NJ + r], 1, 0)
                        q[t, k, NJ + 2 + r] = pltpu.roll(q[t, k, 2 + r], NS - 1, 0)

    squeeze(0, range(NJ // 2))
    squeeze_static()
    first_sends()
    wrap_rows(q0)

    def mirror(x):
        return jnp.take_along_axis(x, NL - 1 - lane, axis=1)

    def levels(kk):
        return pl.ds(NS * kk, NS)

    def fold(step):
        @pl.when(top)
        def _():
            for t in range(2):
                for kk in range(NK // NS):
                    lv = levels(kk)
                    near = mirror(rhal[step, NORTH, t, 1, lv, :])
                    far = mirror(rhal[step, NORTH, t, 0, lv, :])
                    rhal[step, NORTH, t, 0, lv, :] = near
                    rhal[step, NORTH, t, 1, lv, :] = far
            if step == 0:
                for kk in range(NK // NS):
                    rkh[NORTH, levels(kk), :] = mirror(rkh[NORTH, levels(kk), :])
                for h in (hs, hb):
                    near = mirror(jnp.broadcast_to(h[NORTH, 1:2, :], (NS, NL)))
                    far = mirror(jnp.broadcast_to(h[NORTH, 0:1, :], (NS, NL)))
                    h[NORTH, 0:1, :] = near[0:1]
                    h[NORTH, 1:2, :] = far[0:1]

    def row_static():
        def line(x):
            return jnp.broadcast_to(x, (NS, NL))

        def halo_floor(slot, r):
            return line((hs[slot, r : r + 1, :] * hb[slot, r : r + 1, :]).astype(F32))

        south_floors = [
            jnp.where(low, halo_floor(SOUTH, 0), 0.0),
            jnp.where(low, halo_floor(SOUTH, 1), 0.0),
            line(flb[2, 0:1, :]),
            line(flb[3, 0:1, :]),
        ]
        north_floors = [
            line(flb[NJ, NS - 1 : NS, :]),
            line(flb[NJ + 1, NS - 1 : NS, :]),
            halo_floor(NORTH, 0),
            halo_floor(NORTH, 1),
        ]
        for kk in range(NK // NS):
            lv = levels(kk)
            depth = (sub + NS * kk).astype(F32)
            for side, floors in ((SOUTH, south_floors), (NORTH, north_floors)):
                if side == SOUTH:
                    v = jnp.where(low, rvh[SOUTH, lv, :], 0.0)
                    ka, kc = jnp.where(low, rkh[SOUTH, lv, :], 0.0), rk[0, lv, :]
                    inner = rv[0, lv, :]
                    keep = inner > 0
                else:
                    v = rv[2, lv, :]
                    ka, kc = rk[1, lv, :], rkh[NORTH, lv, :]
                    inner = rv[1, lv, :]
                    keep = inner <= 0
                for n in range(3):
                    is_open = jnp.minimum(floors[n], floors[n + 1]) > depth
                    rcoef[side, n, lv, :] = jnp.where(is_open, 4.0, 0.0)
                    if n == 1:
                        rcoef[side, 3, lv, :] = jnp.where(is_open, v, 0.0)
                rcoef[side, 4, lv, :] = jnp.minimum(0.25 * v, 0.0) - 0.125 * (ka + kc)
                rcoef[side, 5, lv, :] = quarter_edge(v)
                rcoef[side, 6, lv, :] = jnp.where(keep, quarter_edge(inner), 0.0)

    def row_correction(step):
        for t in range(2):
            for kk in range(NK // NS):
                lv = levels(kk)
                for side in (SOUTH, NORTH):
                    own = [rown[step, t, 2 * side + r, lv, :] for r in range(2)]
                    if side == SOUTH:
                        halo = [jnp.where(low, rhal[step, SOUTH, t, r, lv, :], 0.0) for r in range(2)]
                        w = halo + own
                    else:
                        halo = [rhal[step, NORTH, t, r, lv, :] for r in range(2)]
                        w = own + halo
                    d = [(w[n + 1] - w[n]) * rcoef[side, n, lv, :] for n in range(3)]
                    h1 = limiter(w[2] - w[0], d[0], d[1])
                    h2 = limiter(w[3] - w[1], d[1], d[2])
                    s = rcoef[side, 3, lv, :]
                    f = s * w[1] + rcoef[side, 4, lv, :] * d[1] + rcoef[side, 5, lv, :] * jnp.where(s > 0, h1, h2)
                    g = rcoef[side, 6, lv, :] * (h2 if side == SOUTH else h1)
                    if side == SOUTH:
                        rc[t, 0, lv, :] = f - g
                        rc[t, 1, lv, :] = g
                    else:
                        rc[t, 2, lv, :] = -g
                        rc[t, 3, lv, :] = g - f

    def add_rows(out, off):
        @pl.loop(0, NK // 4)
        def _(kk):
            for k4 in range(4):
                k = 4 * kk + k4
                for a, (j, s) in enumerate(((0, 0), (1, 0), (NJ - 2, NS - 1), (NJ - 1, NS - 1))):
                    for t in range(2):
                        out[t, k, j + off, s : s + 1, :] = (
                            out[t, k, j + off, s : s + 1, :] + rc[t, a, pl.ds(k, 1), :]
                        )

    def wait_rows(slot):
        for copy in row_copies(0, 0, slot, 0, north):
            copy.wait_recv()

    level4 = (group & (NK - 1)).astype(F32)

    def edge_static():
        @pl.loop(0, NJ // 4)
        def _(quarter):
          for h in range(4):
            j = 4 * quarter + h
            index = 4 * j + l4

            def spread(x):
                return jnp.take_along_axis(x, index, axis=1)

            own_f, east_f, west_f = spread(flo[...]), spread(flr[EAST]), spread(flr[WEST])

            level = group & (NK - 1)
            west_uk = got_uk[j & 3]
            west_at = 32 * (j >> 2) + level
            west_u = jnp.take_along_axis(west_uk, west_at, axis=1)
            west_k = jnp.take_along_axis(west_uk, west_at + NK, axis=1)
            east_k = jnp.take_along_axis(got_k[j & 1], NK * (j >> 1) + level, axis=1)

            def halves(x):
                other = pltpu.roll(x, NL // 2, 1)
                return jnp.where(lane < NL // 2, x, other), jnp.where(lane < NL // 2, other, x)

            own_u, own_k = halves(uko[j])
            first = l4 < 2
            for side in (EAST, WEST):
                if side == EAST:
                    floor, u, kap = jnp.where(first, own_f, east_f), own_u, jnp.where(first, own_k, east_k)
                else:
                    floor, u, kap = (
                        jnp.where(first, west_f, own_f),
                        jnp.where(first, west_u, own_u),
                        jnp.where(first, west_k, own_k),
                    )
                face = jnp.minimum(floor, pltpu.roll(floor, NL - 1, 1))
                is_open = (face > level4) & (l4 < 3)
                b = jnp.minimum(0.25 * u, 0.0) - 0.125 * (kap + pltpu.roll(kap, NL - 1, 1))
                e = quarter_edge(u)
                outer = l4 == 1
                eo[side, j] = jnp.where(is_open, 4.0, 0.0)
                es[side, j] = jnp.where(is_open & outer, u, 0.0)
                eb[side, j] = jnp.where(outer, b, 0.0)
                if side == EAST:
                    c_lanes, d_lanes = outer, first
                else:
                    c_lanes, d_lanes = (l4 == 1) | (l4 == 2), outer
                ec[side, j] = jnp.where((u > 0) & c_lanes, e, 0.0)
                ed[side, j] = jnp.where((u <= 0) & d_lanes, e, 0.0)

    def edge_correction(step, j):
        own = pq[step, j]
        first = l4 < 2
        sums = []
        at = 2 * group + (lane & 1) + (NL // 2 if j >= NJ // 2 else 0)
        a = j % (NJ // 2)
        for side in (EAST, WEST):
            if side == EAST:
                win = jnp.where(first, own, jnp.take_along_axis(pr[step, EAST, a], at, axis=1))
            else:
                win = jnp.where(first, jnp.take_along_axis(pr[step, WEST, a], at, axis=1), own)
            d = (pltpu.roll(win, NL - 1, 1) - win) * eo[side, j]
            before = pltpu.roll(d, 1, 1)
            h = limiter(0.25 * (d + before), before, d)
            g = es[side, j] * win + eb[side, j] * d + ec[side, j] * h + ed[side, j] * pltpu.roll(h, NL - 1, 1)
            sums.append(pltpu.roll(g, 1, 1) - g)
        cc[j] = jnp.where(first, sums[EAST], sums[WEST])

    def edge_corrections(step):
        for j in range(NJ):
            edge_correction(step, j)

    def unpacked(j, n):
        return jnp.where(edge_lanes, pltpu.roll(cc[j], (NL - 2 - 4 * n) % NL, 1), 0.0)

    def add_columns(out, off, j):
        for t in range(2):
            for k in range(NK):
                out[t, k, j + off] = out[t, k, j + off] + unpacked(j, NK * t + k)

    def zonal_slopes(q, j, slot):
        for k in range(NK):
            o, ow = ox[k, j], oxw[k, j]
            for t in range(2):
                x = q[t, k, j + 2]
                after = pltpu.roll(x, NL - 1, 1)
                before = pltpu.roll(x, 1, 1)
                d = (after - x) * o
                dx[slot, t, k] = d
                hx[slot, t, k] = limiter(after - before, (x - before) * ow, d)

    def zonal_fluxes(q, j, slot):
        for k in range(NK):
            s, b, e = sx[k, j], bx[k, j], ex[k, j]
            up = s > 0
            for t in range(2):
                x, d, h = q[t, k, j + 2], dx[slot, t, k], hx[slot, t, k]
                fx[slot, t, k] = s * x + b * d + e * jnp.where(up, h, pltpu.roll(h, NL - 1, 1))

    def repack(out, off, j):
        sums = []
        for t in range(2):
            for k in range(NK):
                n = NK * t + k
                moved = pltpu.roll(jnp.where(edge_lanes, out[t, k, j + off], 0.0), (4 * n + 2) % NL, 1)
                if len(sums) < 4:
                    sums.append(moved)
                else:
                    sums[n % 4] = sums[n % 4] + moved
        pq[1, j] = (sums[0] + sums[1]) + (sums[2] + sums[3])

    def meridional_start(q, j):
        @pl.loop(0, NK // 4)
        def _(kk):
            for k4 in range(4):
                k = 4 * kk + k4
                s, b, e = sy[k, j], by[k, j], ey[k, j]
                for t in range(2):
                    a2, a1, c0, c1 = (q[t, k, j + n] for n in range(4))
                    d2 = (a1 - a2) * oy[k, j]
                    d1 = (c0 - a1) * oy[k, j + 1]
                    d0 = (c1 - c0) * oy[k, j + 2]
                    h1 = limiter(c0 - a2, d2, d1)
                    h0 = limiter(c1 - a1, d1, d0)
                    dy[t, k] = d0
                    hy[t, k] = h0
                    fy[t, k] = s * a1 + b * d1 + e * jnp.where(s > 0, h1, h0)

    def rest(q, out, off, j, step, slot, fix):
        fl = flb[j + 2]
        state = []
        for t in range(2):
            x0, x1 = q[t, 0, j + 2], q[t, 1, j + 2]
            d0 = (x1 - x0) * oz[0, j]
            state.append([x0, x1, d0, None, None])
        for k in range(NK):
            s, b, e = sy[k, j + 1], by[k, j + 1], ey[k, j + 1]
            up = s > 0
            oy1 = oy[k, j + 3]
            if k < NK - 1:
                zs, ze = sz[k, j], ez[k, j]
                zup = zs > 0
            if k < NK - 2:
                zo = oz[k + 1, j]
            wet = fl > k
            for t in range(2):
                x, below, zd, zh, zf = state[t]
                y1, y2 = q[t, k, j + 3], q[t, k, j + 4]
                d0, h0 = dy[t, k], hy[t, k]
                d1 = (y2 - y1) * oy1
                h1 = limiter(y2 - x, d0, d1)
                f = s * x + b * d0 + e * jnp.where(up, h0, h1)
                flux = fx[slot, t, k]
                acc = (pltpu.roll(flux, 1, 1) - flux) + (fy[t, k] - f)
                if fix:
                    acc = acc + unpacked(j, NK * t + k)
                dy[t, k] = d1
                hy[t, k] = h1
                fy[t, k] = f
                if k < NK - 1:
                    if k < NK - 2:
                        deeper = q[t, k + 2, j + 2]
                        zd1 = (deeper - below) * zo
                        zh1 = limiter(deeper - x, zd, zd1)
                    else:
                        deeper, zd1, zh1 = None, None, None
                    slope_near = 0.0 if zh is None else zh
                    slope_far = 0.0 if zh1 is None else zh1
                    nf = zs * jnp.where(zup, x, below) + ze * jnp.where(zup, slope_near, slope_far)
                    acc = acc - nf
                    state[t] = [below, deeper, zd1, zh1, nf]
                if zf is not None:
                    acc = acc + zf
                if step == 0:
                    new = jnp.where(wet, x, 0.0) + acc
                else:
                    new = x + acc
                out[t, k, j + off] = new

    def sweep(q, out, off, step, first, last, repacking, fixing_in, fixing_out, at_start):
        @pl.loop(first, last)
        def _(i):
            at_start(i)

            for half in range(2):
                j = (2 * i + 2 + half) & (NJ - 1)
                if repacking:
                    repack(out, off, (j - 1) & (NJ - 1))
                rest(q, out, off, j, step, half, fixing_out)
                zonal_fluxes(q, (j + 1) & (NJ - 1), 1 - half)
                zonal_slopes(q, (j + 2) & (NJ - 1), half)
                if fixing_in:
                    add_columns(q, 2, j + 3)
                if fixing_out:
                    add_columns(out, off, (j - NJ // 2) & (NJ - 1))

    def start_sweep(q):
        zonal_slopes(q, 2, 0)
        zonal_slopes(q, 3, 1)
        zonal_fluxes(q, 2, 0)
        meridional_start(q, 2)

    def restart(q):
        def at(i):
            @pl.when(i == 7)
            def _():
                meridional_start(q, 0)

        return at

    start_sweep(q0)
    sweep(q0, q1, 2, 0, 0, 8, True, False, False, restart(q0))

    for copy in own_row_copies():
        copy.wait()
    wait_rows(NORTH)

    @pl.when(low)
    def _():
        wait_rows(SOUTH)

    fold(0)
    row_static()
    row_correction(0)
    for copy in static_col_copies():
        copy.wait_recv()
    for copy in col_copies(0, 0):
        copy.wait_recv()
    edge_static()
    edge_corrections(0)
    for j in range(2, NJ - 2):
        pq[1, j] = pq[1, j] + cc[j]
    squeeze(1, range(2, NJ // 2 - 2))
    for copy in col_copies(1, 0):
        copy.start()
    add_rows(q1, 2)

    @pl.loop(0, 2)
    def _(half):
        for h in range(2):
            add_columns(q1, 2, (2 * half + h + NJ - 2) & (NJ - 1))


    def row2_copies(j, s, slot, direction, device):
        return [
            remote(
                q1.at[t, :, j + r + 2, s, :], rhal.at[1, slot, t, r],
                row2_send.at[direction, t, r], row2_recv.at[slot, t, r], device,
            )
            for t in range(2)
            for r in range(2)
        ]

    def north2(slot):
        return row2_copies(NJ - 2, NS - 1, slot, 0, north)

    def south2():
        return row2_copies(0, 0, NORTH, 1, south)

    def own2_copies():
        return [
            pltpu.make_async_copy(q1.at[t, :, j + 2, s, :], rown.at[1, t, a], own2_sem.at[t, a])
            for t in range(2)
            for a, (j, s) in enumerate(((0, 0), (1, 0), (NJ - 2, NS - 1), (NJ - 1, NS - 1)))
        ]

    for copy in north2(nslot):
        copy.start()

    @pl.when(low)
    def _():
        for copy in south2():
            copy.start()

    for copy in own2_copies():
        copy.start()

    @pl.loop(0, 2)
    def _(half):
        for h in range(2):
            repack(q1, 2, (2 * half + h + NJ - 2) & (NJ - 1))

    squeeze(1, (0, 1, NJ // 2 - 2, NJ // 2 - 1))
    for part in (1, 2):
        for copy in col_copies(1, part):
            copy.start()

    @pl.loop(0, 2)
    def _(half):
        for h in range(2):
            add_columns(q1, 2, 2 + h + half * (2 + 8 * h))

    wrap_rows(q1)
    start_sweep(q1)
    sweep(q1, ob, 0, 1, 0, 4, False, True, False, lambda i: None)

    for copy in own2_copies():
        copy.wait()
    for copy in north2(NORTH):
        copy.wait_recv()

    @pl.when(low)
    def _():
        for copy in north2(SOUTH):
            copy.wait_recv()

    fold(1)
    row_correction(1)
    for part in range(3):
        for copy in col_copies(1, part):
            copy.wait_recv()
    edge_corrections(1)

    OUTS = (2, 4), (10, 4), (6, 4), (14, 2), (0, 2)

    def out_start(part):
        first, size = OUTS[part]

        @pl.loop(0, NS)
        def _(s):
            for t, dst in enumerate((tout_hbm, sout_hbm)):
                pltpu.make_async_copy(
                    ob.at[t, :, pl.ds(first, size), s, :],
                    dst.at[:, pl.ds(NJ * s + first, size), :],
                    out_sem.at[t, part],
                ).start()

    def out_wait(part):
        first, size = OUTS[part]
        for t in range(2):
            whole = ob.at[t, :, pl.ds(first, size)]
            pltpu.make_async_copy(whole, whole, out_sem.at[t, part]).wait()

    def at_start(i):
        @pl.when(i == 6)
        def _():
            for part in range(2):
                out_start(part)

        restart(q1)(i)

    sweep(q1, ob, 0, 1, 4, 8, False, False, True, at_start)
    out_start(2)
    add_rows(ob, 0)
    for part in (3, 4):
        out_start(part)

    for copy in north_rows(nslot) + north2(nslot):
        copy.wait_send()

    @pl.when(low)
    def _():
        for copy in south_rows() + south2():
            copy.wait_send()

    for copy in static_col_copies():
        copy.wait_send()
    for step in range(2):
        for part in range(len(PARTS[step])):
            for copy in col_copies(step, part):
                copy.wait_send()
    for part in range(len(OUTS)):
        out_wait(part)


def hand_over(t_in, s_in, t_out, s_out, held, in_sem, out_sem):
    pieces = [
        (src.at[pl.ds(4 * n, 4)], held.at[a, pl.ds(4 * n, 4)], dst.at[pl.ds(4 * n, 4)], a, n)
        for n in range(4)
        for a, (src, dst) in enumerate(((t_in, t_out), (s_in, s_out)))
    ]
    reads = [pltpu.make_async_copy(src, mid, in_sem.at[a, n]) for src, mid, dst, a, n in pieces]
    writes = [pltpu.make_async_copy(mid, dst, out_sem.at[a, n]) for src, mid, dst, a, n in pieces]
    for copy in reads:
        copy.start()
    for read, write in zip(reads, writes):
        read.wait()
        write.start()
    for copy in writes:
        copy.wait()


def on_device(t, s, u, v, w, kap, sea, bot):
    def vm(*lead):
        return pltpu.VMEM(lead + (NS, NL), F32)

    def rows(*lead):
        return pltpu.VMEM(lead + (NK, NL), F32)

    def vi(*lead):
        return pltpu.VMEM(lead + (NS, NL), jnp.int32)

    dma = pltpu.SemaphoreType.DMA
    anywhere = pl.BlockSpec(memory_space=pl.ANY)
    shape = jax.ShapeDtypeStruct(t.shape, F32)
    held = pl.pallas_call(
        kernel,
        out_shape=(shape, shape),
        in_specs=[anywhere] * 8,
        out_specs=(anywhere, anywhere),
        scratch_shapes=[
            vm(2, NK, NJ + 4), vm(2, NK, NJ + 4), vm(2, NK, NJ),
            vm(NK, NJ), vm(NK, NJ), vm(NK, NJ + 1), vm(NK, NJ + 2),
            vi(NJ + 4), vi(NJ + 4), vm(NJ + 4),
            vm(NK, NJ), vm(NK, NJ), vm(NK, NJ), vm(NK, NJ),
            vm(NK, NJ + 3), vm(NK, NJ + 1), vm(NK, NJ + 1), vm(NK, NJ + 1),
            vm(NK, NJ), vm(NK, NJ), vm(NK, NJ),
            vm(NK, NJ), vm(2, 2, NK), vm(2, 2, NK), vm(2, 2, NK), vm(2, NK), vm(2, NK), vm(2, NK),
            rows(2, 2, 4), rows(2, 2, 2, 2), rows(2), rows(2), rows(3), rows(2),
            pltpu.VMEM((2, 2, NL), jnp.int32), pltpu.VMEM((2, 2, NL), jnp.int32), rows(2, 7), rows(2, 4),
            vm(2, NJ), vm(2, 2, NJ // 2), vm(2, 2, NJ // 2), vm(NJ), vm(4), vm(4), vm(2), vm(2), vm(), vm(2), vm(NJ),
            vm(2, NJ), vm(2, NJ), vm(2, NJ), vm(2, NJ), vm(2, NJ),
            dma((8,)), dma((13,)), dma((2, 4)), dma((2, 5)), dma((2, 8)), dma((2, 8)), dma((2, 2, 2)), dma((2, 2, 2)),
            dma((2, 2)), dma((2, 2)), dma((2, 2, 3)), dma((2, 2, 3)),
        ],
        compiler_params=pltpu.CompilerParams(
            collective_id=0, has_side_effects=True, vmem_limit_bytes=58 * 1024 * 1024
        ),
        cost_estimate=pl.CostEstimate(flops=120_000_000, bytes_accessed=9_000_000, transcendentals=0),
    )(t, s, u, v, w, kap, sea, bot)
    return pl.pallas_call(
        hand_over,
        out_shape=(shape, shape),
        in_specs=[anywhere] * 2,
        out_specs=(anywhere, anywhere),
        scratch_shapes=[pltpu.VMEM((2,) + t.shape, F32), dma((2, 4)), dma((2, 4))],
        compiler_params=pltpu.CompilerParams(vmem_limit_bytes=60 * 1024 * 1024),
    )(*held)


def solution(mesh):
    block = P(None, "ja", "ia")
    flat = P("ja", "ia")
    return jax.shard_map(
        on_device,
        mesh=mesh,
        in_specs=(block,) * 6 + (flat, flat),
        out_specs=(block, block),
        check_vma=False,
    )
```

```python
import jax
import jax.numpy as jnp
from jax import lax
from jax.experimental import pallas as pl
from jax.experimental.pallas import tpu as pltpu
from jax.sharding import PartitionSpec as P

NK = 16
NJ = 16
NS = 8
NL = 128
F32 = jnp.float32
EAST, WEST = 0, 1
SOUTH, NORTH = 0, 1


def limiter(centred, a, b):
    upper = jnp.maximum(jnp.minimum(a, b), 0.0)
    lower = jnp.minimum(jnp.maximum(a, b), 0.0)
    return jnp.maximum(jnp.minimum(centred, upper), lower)


def quarter_edge(s):
    a = jnp.abs(s)
    return a * (0.25 - 0.25 * a)


def kernel(
    t_hbm, s_hbm, u_hbm, v_hbm, w_hbm, k_hbm, sea_hbm, bot_hbm,
    tout_hbm, sout_hbm,
    q0, q1, ob, ub, wb, vb, kb, seab, botb, flb,
    ox, sx, bx, ex, oy, sy, by, ey, oz, sz, ez,
    oxw, dx, hx, fx, dy, hy, fy,
    rown, rhal, rk, rkh, rv, rvh, hs, hb, rcoef, rc,
    pq, pr, sent, uko, sent_uk, got_uk, sent_k, got_k, flo, flr, cc,
    eo, es, eb, ec, ed,
    in_sem, own_sem, own2_sem, out_sem, row_send, row_recv, row2_send, row2_recv,
    col_send, col_recv, col2_send, col2_recv,
):
    ia = lax.axis_index("ia")
    ja = lax.axis_index("ja")
    n_ia = lax.axis_size("ia")
    n_ja = lax.axis_size("ja")
    top = ja == n_ja - 1
    low = ja > 0
    east = {"ia": lax.rem(ia + 1, n_ia), "ja": ja}
    west = {"ia": lax.rem(ia + n_ia - 1, n_ia), "ja": ja}
    north = {"ia": jnp.where(top, n_ia - 1 - ia, ia), "ja": jnp.where(top, ja, ja + 1)}
    south = {"ia": ia, "ja": jnp.maximum(ja - 1, 0)}
    nslot = jnp.where(top, NORTH, SOUTH)
    mesh_ids = pl.DeviceIdType.MESH

    lane = lax.broadcasted_iota(jnp.int32, (NS, NL), 1)
    sub = lax.broadcasted_iota(jnp.int32, (NS, NL), 0)
    l4 = lane & 3
    group = lane >> 2
    edge_lanes = ((lane + 2) & (NL - 1)) < 4

    barrier = pltpu.get_barrier_semaphore()
    for device in (east, west, north):
        pl.semaphore_signal(barrier, inc=1, device_id=device, device_id_type=mesh_ids)

    @pl.when(low)
    def _():
        pl.semaphore_signal(barrier, inc=1, device_id=south, device_id_type=mesh_ids)

    @pl.loop(0, NS)
    def _(s):
        rows = pl.ds(pl.multiple_of(NJ * s, NJ), NJ)
        inner = pl.ds(2, NJ)
        inner1 = pl.ds(1, NJ)
        for index, (src, dst) in enumerate((
            (t_hbm.at[:, rows, :], q0.at[0, :, inner, s, :]),
            (s_hbm.at[:, rows, :], q0.at[1, :, inner, s, :]),
            (sea_hbm.at[rows, :], seab.at[inner, s, :]),
            (bot_hbm.at[rows, :], botb.at[inner, s, :]),
            (u_hbm.at[:, rows, :], ub.at[:, :, s, :]),
            (k_hbm.at[:, rows, :], kb.at[:, inner1, s, :]),
            (v_hbm.at[:, rows, :], vb.at[:, inner1, s, :]),
            (w_hbm.at[:, rows, :], wb.at[:, :, s, :]),
        )):
            pltpu.make_async_copy(src, dst, in_sem.at[index]).start()

    def loaded(index, whole):
        pltpu.make_async_copy(whole, whole, in_sem.at[index]).wait()

    rows_total = NJ * NS
    edge_rows = (0, 1, rows_total - 2, rows_total - 1)

    def own_row_copies():
        pairs = [
            (src.at[:, row, :], rown.at[0, t, a])
            for t, src in enumerate((t_hbm, s_hbm))
            for a, row in enumerate(edge_rows)
        ]
        pairs += [(k_hbm.at[:, row, :], rk.at[a]) for a, row in enumerate((0, rows_total - 1))]
        pairs += [(v_hbm.at[:, row, :], rv.at[a]) for a, row in enumerate((0, rows_total - 2, rows_total - 1))]
        return [pltpu.make_async_copy(a, b, own_sem.at[n]) for n, (a, b) in enumerate(pairs)]

    for copy in own_row_copies():
        copy.start()

    def remote(src, dst, ssem, rsem, device):
        return pltpu.make_async_remote_copy(
            src_ref=src, dst_ref=dst, send_sem=ssem, recv_sem=rsem,
            device_id=device, device_id_type=mesh_ids,
        )

    def row_copies(first, last, slot, direction, device):
        pair = pl.ds(first, 2)
        parts = [
            (src.at[:, first + r, :], rhal.at[0, slot, t, r])
            for t, src in enumerate((t_hbm, s_hbm))
            for r in range(2)
        ] + [
            (k_hbm.at[:, last, :], rkh.at[slot]),
            (v_hbm.at[:, last, :], rvh.at[slot]),
            (sea_hbm.at[pair, :], hs.at[slot]),
            (bot_hbm.at[pair, :], hb.at[slot]),
        ]
        return [
            remote(src, dst, row_send.at[direction, n], row_recv.at[slot, n], device)
            for n, (src, dst) in enumerate(parts)
        ]

    def north_rows(slot):
        return row_copies(rows_total - 2, rows_total - 1, slot, 0, north)

    def south_rows():
        return row_copies(0, 0, NORTH, 1, south)

    def pack(load_vreg, count):
        acc = jnp.zeros((NS, NL), F32)
        for n in range(count):
            moved = pltpu.roll(load_vreg(n), (4 * n + 2) % NL, 1)
            acc = jnp.where(group == n, moved, acc)
        return acc

    PARTS = ((0, NJ // 2),), ((2, NJ // 2 - 4), (NJ // 2 - 2, 2), (0, 2))

    def squeeze(step, rows):
        pair = lane & 63
        index = 4 * (pair >> 1) + (pair & 1)
        first = lane < NL // 2
        for a in rows:
            for side in (EAST, WEST):
                at = index + (2 if side == WEST else 0)
                sent[step, side, a] = jnp.where(
                    first,
                    jnp.take_along_axis(pq[step, a], at, axis=1),
                    jnp.take_along_axis(pq[step, a + NJ // 2], at, axis=1),
                )

    def col_copies(step, part):
        first, size = PARTS[step][part]
        sl = pl.ds(first, size)
        return [
            remote(sent.at[step, WEST, sl], pr.at[step, EAST, sl], col2_send.at[step, 0, part], col2_recv.at[step, EAST, part], west),
            remote(sent.at[step, EAST, sl], pr.at[step, WEST, sl], col2_send.at[step, 1, part], col2_recv.at[step, WEST, part], east),
        ]

    def squeeze_static():
        quarter = lane & 31
        to_east = 4 * quarter + 1
        to_west = NL // 2 + 4 * (lane & 15) + 2
        for m in range(4):
            acc = jnp.take_along_axis(uko[m], to_east, axis=1)
            for n in range(1, 4):
                acc = jnp.where((lane >> 5) == n, jnp.take_along_axis(uko[m + 4 * n], to_east, axis=1), acc)
            sent_uk[m] = acc
        for m in range(2):
            acc = jnp.take_along_axis(uko[m], to_west, axis=1)
            for n in range(1, 8):
                acc = jnp.where((lane >> 4) == n, jnp.take_along_axis(uko[m + 2 * n], to_west, axis=1), acc)
            sent_k[m] = acc

    def static_col_copies():
        return [
            remote(sent_k, got_k, col_send.at[0, 0], col_recv.at[EAST, 0], west),
            remote(sent_uk, got_uk, col_send.at[1, 0], col_recv.at[WEST, 0], east),
            remote(flo, flr.at[EAST], col_send.at[0, 1], col_recv.at[EAST, 1], west),
            remote(flo, flr.at[WEST], col_send.at[1, 1], col_recv.at[WEST, 1], east),
        ]

    loaded(0, q0.at[0, :, pl.ds(2, NJ)])
    loaded(1, q0.at[1, :, pl.ds(2, NJ)])

    @pl.loop(0, NJ // 2)
    def _(half):
        for h in range(2):
            j = 2 * half + h
            pq[0, j] = pack(lambda n: q0[n // NK, n % NK, j + 2], 2 * NK)

    loaded(2, seab.at[pl.ds(2, NJ)])
    loaded(3, botb.at[pl.ds(2, NJ)])
    for j in range(2, NJ + 2):
        flb[j] = (seab[j] * botb[j]).astype(F32)
    flo[...] = pack(lambda n: flb[n + 2], NJ)
    loaded(4, ub)
    loaded(5, kb.at[:, pl.ds(1, NJ)])

    def first_sends():
        pl.semaphore_wait(barrier, jnp.where(low, 4, 3))
        for copy in col_copies(0, 0):
            copy.start()
        for copy in north_rows(nslot):
            copy.start()

        @pl.when(low)
        def _():
            for copy in south_rows():
                copy.start()

    squeeze(0, range(NJ // 2))

    loaded(6, vb.at[:, pl.ds(1, NJ)])
    loaded(7, wb)

    def open_y(j):
        face = jnp.minimum(flb[j + 2], flb[j + 3])
        for k in range(NK):
            oy[k, j + 2] = jnp.where(face > k, 4.0, 0.0)

    def coef_y(j):
        face = jnp.minimum(flb[j + 2], flb[j + 3])
        for k in range(NK):
            v = vb[k, j + 1]
            sy[k, j + 1] = jnp.where(face > k, v, 0.0)
            by[k, j + 1] = jnp.minimum(0.25 * v, 0.0) - 0.125 * (kb[k, j + 1] + kb[k, j + 2])
            ey[k, j + 1] = quarter_edge(v)

    @pl.loop(0, NJ)
    def _(j):
        @pl.when(j == NJ // 2)
        def _():
            first_sends()

        fl = flb[j + 2]
        face = jnp.where(lane == NL - 1, 0.0, jnp.minimum(fl, pltpu.roll(fl, NL - 1, 1)))
        uko[j] = pack(lambda n: ub[n, j] if n < NK else kb[n - NK, j + 1], 2 * NK)
        face_w = jnp.where(lane == 0, 0.0, jnp.minimum(fl, pltpu.roll(fl, 1, 1)))
        for k in range(NK):
            is_open = face > k
            u = ub[k, j]
            kap = kb[k, j + 1]
            ox[k, j] = jnp.where(is_open, 4.0, 0.0)
            oxw[k, j] = jnp.where(face_w > k, 4.0, 0.0)
            sx[k, j] = jnp.where(is_open, u, 0.0)
            bx[k, j] = jnp.minimum(0.25 * u, 0.0) - 0.125 * (kap + pltpu.roll(kap, NL - 1, 1))
            ex[k, j] = quarter_edge(u)
            if k < NK - 1:
                below = fl > k + 1
                w = wb[k, j]
                oz[k, j] = jnp.where(below, 4.0, 0.0)
                sz[k, j] = jnp.where(below, w, 0.0)
                ez[k, j] = quarter_edge(w)

    squeeze_static()
    for copy in static_col_copies():
        copy.start()

    for r in range(2):
        flb[r] = jnp.where(sub == 0, 0.0, pltpu.roll(flb[NJ + r], 1, 0))
        flb[NJ + 2 + r] = jnp.where(sub == NS - 1, 0.0, pltpu.roll(flb[2 + r], NS - 1, 0))
    for k in range(NK):
        kb[k, 0] = pltpu.roll(kb[k, NJ], 1, 0)
        kb[k, NJ + 1] = pltpu.roll(kb[k, 1], NS - 1, 0)
        vb[k, 0] = pltpu.roll(vb[k, NJ], 1, 0)

    @pl.loop(0, NJ + 1)
    def _(j):
        open_y(j - 1)
        coef_y(j - 1)

    @pl.loop(0, 2)
    def _(r):
        open_y((NJ + 2) * r - 2)

    def wrap_rows(q):
        @pl.loop(0, NK // 4)
        def _(kk):
            for k4 in range(4):
                k = 4 * kk + k4
                for t in range(2):
                    for r in range(2):
                        q[t, k, r] = pltpu.roll(q[t, k, NJ + r], 1, 0)
                        q[t, k, NJ + 2 + r] = pltpu.roll(q[t, k, 2 + r], NS - 1, 0)

    wrap_rows(q0)

    def mirror(x):
        return jnp.take_along_axis(x, NL - 1 - lane, axis=1)

    def levels(kk):
        return pl.ds(NS * kk, NS)

    def fold(step):
        @pl.when(top)
        def _():
            for t in range(2):
                for kk in range(NK // NS):
                    lv = levels(kk)
                    near = mirror(rhal[step, NORTH, t, 1, lv, :])
                    far = mirror(rhal[step, NORTH, t, 0, lv, :])
                    rhal[step, NORTH, t, 0, lv, :] = near
                    rhal[step, NORTH, t, 1, lv, :] = far
            if step == 0:
                for kk in range(NK // NS):
                    rkh[NORTH, levels(kk), :] = mirror(rkh[NORTH, levels(kk), :])
                for h in (hs, hb):
                    near = mirror(jnp.broadcast_to(h[NORTH, 1:2, :], (NS, NL)))
                    far = mirror(jnp.broadcast_to(h[NORTH, 0:1, :], (NS, NL)))
                    h[NORTH, 0:1, :] = near[0:1]
                    h[NORTH, 1:2, :] = far[0:1]

    def row_static():
        def line(x):
            return jnp.broadcast_to(x, (NS, NL))

        def halo_floor(slot, r):
            return line((hs[slot, r : r + 1, :] * hb[slot, r : r + 1, :]).astype(F32))

        south_floors = [
            jnp.where(low, halo_floor(SOUTH, 0), 0.0),
            jnp.where(low, halo_floor(SOUTH, 1), 0.0),
            line(flb[2, 0:1, :]),
            line(flb[3, 0:1, :]),
        ]
        north_floors = [
            line(flb[NJ, NS - 1 : NS, :]),
            line(flb[NJ + 1, NS - 1 : NS, :]),
            halo_floor(NORTH, 0),
            halo_floor(NORTH, 1),
        ]
        for kk in range(NK // NS):
            lv = levels(kk)
            depth = (sub + NS * kk).astype(F32)
            for side, floors in ((SOUTH, south_floors), (NORTH, north_floors)):
                if side == SOUTH:
                    v = jnp.where(low, rvh[SOUTH, lv, :], 0.0)
                    ka, kc = jnp.where(low, rkh[SOUTH, lv, :], 0.0), rk[0, lv, :]
                    inner = rv[0, lv, :]
                    keep = inner > 0
                else:
                    v = rv[2, lv, :]
                    ka, kc = rk[1, lv, :], rkh[NORTH, lv, :]
                    inner = rv[1, lv, :]
                    keep = inner <= 0
                for n in range(3):
                    is_open = jnp.minimum(floors[n], floors[n + 1]) > depth
                    rcoef[side, n, lv, :] = jnp.where(is_open, 4.0, 0.0)
                    if n == 1:
                        rcoef[side, 3, lv, :] = jnp.where(is_open, v, 0.0)
                rcoef[side, 4, lv, :] = jnp.minimum(0.25 * v, 0.0) - 0.125 * (ka + kc)
                rcoef[side, 5, lv, :] = quarter_edge(v)
                rcoef[side, 6, lv, :] = jnp.where(keep, quarter_edge(inner), 0.0)

    def row_correction(step):
        for t in range(2):
            for kk in range(NK // NS):
                lv = levels(kk)
                for side in (SOUTH, NORTH):
                    own = [rown[step, t, 2 * side + r, lv, :] for r in range(2)]
                    if side == SOUTH:
                        halo = [jnp.where(low, rhal[step, SOUTH, t, r, lv, :], 0.0) for r in range(2)]
                        w = halo + own
                    else:
                        halo = [rhal[step, NORTH, t, r, lv, :] for r in range(2)]
                        w = own + halo
                    d = [(w[n + 1] - w[n]) * rcoef[side, n, lv, :] for n in range(3)]
                    h1 = limiter(w[2] - w[0], d[0], d[1])
                    h2 = limiter(w[3] - w[1], d[1], d[2])
                    s = rcoef[side, 3, lv, :]
                    f = s * w[1] + rcoef[side, 4, lv, :] * d[1] + rcoef[side, 5, lv, :] * jnp.where(s > 0, h1, h2)
                    g = rcoef[side, 6, lv, :] * (h2 if side == SOUTH else h1)
                    if side == SOUTH:
                        rc[t, 0, lv, :] = f - g
                        rc[t, 1, lv, :] = g
                    else:
                        rc[t, 2, lv, :] = -g
                        rc[t, 3, lv, :] = g - f

    def add_rows(out, off):
        @pl.loop(0, NK // 4)
        def _(kk):
            for k4 in range(4):
                k = 4 * kk + k4
                for a, (j, s) in enumerate(((0, 0), (1, 0), (NJ - 2, NS - 1), (NJ - 1, NS - 1))):
                    for t in range(2):
                        out[t, k, j + off, s : s + 1, :] = (
                            out[t, k, j + off, s : s + 1, :] + rc[t, a, pl.ds(k, 1), :]
                        )

    def wait_rows(slot):
        for copy in row_copies(0, 0, slot, 0, north):
            copy.wait_recv()

    level4 = (group & (NK - 1)).astype(F32)

    def edge_static():
        @pl.loop(0, NJ // 8)
        def _(half):
          for h in range(8):
            j = 8 * half + h
            index = 4 * j + l4

            def spread(x):
                return jnp.take_along_axis(x, index, axis=1)

            own_f, east_f, west_f = spread(flo[...]), spread(flr[EAST]), spread(flr[WEST])

            level = group & (NK - 1)
            west_uk = got_uk[j & 3]
            west_at = 32 * (j >> 2) + level
            west_u = jnp.take_along_axis(west_uk, west_at, axis=1)
            west_k = jnp.take_along_axis(west_uk, west_at + NK, axis=1)
            east_k = jnp.take_along_axis(got_k[j & 1], NK * (j >> 1) + level, axis=1)

            def halves(x):
                other = pltpu.roll(x, NL // 2, 1)
                return jnp.where(lane < NL // 2, x, other), jnp.where(lane < NL // 2, other, x)

            own_u, own_k = halves(uko[j])
            first = l4 < 2
            for side in (EAST, WEST):
                if side == EAST:
                    floor, u, kap = jnp.where(first, own_f, east_f), own_u, jnp.where(first, own_k, east_k)
                else:
                    floor, u, kap = (
                        jnp.where(first, west_f, own_f),
                        jnp.where(first, west_u, own_u),
                        jnp.where(first, west_k, own_k),
                    )
                face = jnp.minimum(floor, pltpu.roll(floor, NL - 1, 1))
                is_open = (face > level4) & (l4 < 3)
                b = jnp.minimum(0.25 * u, 0.0) - 0.125 * (kap + pltpu.roll(kap, NL - 1, 1))
                e = quarter_edge(u)
                outer = l4 == 1
                eo[side, j] = jnp.where(is_open, 4.0, 0.0)
                es[side, j] = jnp.where(is_open & outer, u, 0.0)
                eb[side, j] = jnp.where(outer, b, 0.0)
                if side == EAST:
                    c_lanes, d_lanes = outer, first
                else:
                    c_lanes, d_lanes = (l4 == 1) | (l4 == 2), outer
                ec[side, j] = jnp.where((u > 0) & c_lanes, e, 0.0)
                ed[side, j] = jnp.where((u <= 0) & d_lanes, e, 0.0)

    def edge_correction(step, j):
        own = pq[step, j]
        first = l4 < 2
        sums = []
        at = 2 * group + (lane & 1) + (NL // 2 if j >= NJ // 2 else 0)
        a = j % (NJ // 2)
        for side in (EAST, WEST):
            if side == EAST:
                win = jnp.where(first, own, jnp.take_along_axis(pr[step, EAST, a], at, axis=1))
            else:
                win = jnp.where(first, jnp.take_along_axis(pr[step, WEST, a], at, axis=1), own)
            d = (pltpu.roll(win, NL - 1, 1) - win) * eo[side, j]
            before = pltpu.roll(d, 1, 1)
            h = limiter(0.25 * (d + before), before, d)
            g = es[side, j] * win + eb[side, j] * d + ec[side, j] * h + ed[side, j] * pltpu.roll(h, NL - 1, 1)
            sums.append(pltpu.roll(g, 1, 1) - g)
        cc[j] = jnp.where(first, sums[EAST], sums[WEST])

    def edge_corrections(step):
        for j in range(NJ):
            edge_correction(step, j)

    def unpacked(j, n):
        return jnp.where(edge_lanes, pltpu.roll(cc[j], (NL - 2 - 4 * n) % NL, 1), 0.0)

    def add_columns(out, off, j):
        for t in range(2):
            for k in range(NK):
                out[t, k, j + off] = out[t, k, j + off] + unpacked(j, NK * t + k)

    def zonal_slopes(q, j, slot):
        for k in range(NK):
            o, ow = ox[k, j], oxw[k, j]
            for t in range(2):
                x = q[t, k, j + 2]
                after = pltpu.roll(x, NL - 1, 1)
                before = pltpu.roll(x, 1, 1)
                d = (after - x) * o
                dx[slot, t, k] = d
                hx[slot, t, k] = limiter(after - before, (x - before) * ow, d)

    def zonal_fluxes(q, j, slot):
        for k in range(NK):
            s, b, e = sx[k, j], bx[k, j], ex[k, j]
            up = s > 0
            for t in range(2):
                x, d, h = q[t, k, j + 2], dx[slot, t, k], hx[slot, t, k]
                fx[slot, t, k] = s * x + b * d + e * jnp.where(up, h, pltpu.roll(h, NL - 1, 1))

    def repack(out, off, j):
        sums = []
        for t in range(2):
            for k in range(NK):
                n = NK * t + k
                moved = pltpu.roll(jnp.where(edge_lanes, out[t, k, j + off], 0.0), (4 * n + 2) % NL, 1)
                if len(sums) < 4:
                    sums.append(moved)
                else:
                    sums[n % 4] = sums[n % 4] + moved
        pq[1, j] = (sums[0] + sums[1]) + (sums[2] + sums[3])

    def meridional_start(q, j):
        @pl.loop(0, NK // 8)
        def _(kk):
            for k4 in range(8):
                k = 8 * kk + k4
                s, b, e = sy[k, j], by[k, j], ey[k, j]
                for t in range(2):
                    a2, a1, c0, c1 = (q[t, k, j + n] for n in range(4))
                    d2 = (a1 - a2) * oy[k, j]
                    d1 = (c0 - a1) * oy[k, j + 1]
                    d0 = (c1 - c0) * oy[k, j + 2]
                    h1 = limiter(c0 - a2, d2, d1)
                    h0 = limiter(c1 - a1, d1, d0)
                    dy[t, k] = d0
                    hy[t, k] = h0
                    fy[t, k] = s * a1 + b * d1 + e * jnp.where(s > 0, h1, h0)

    def rest(q, out, off, j, step, slot, fix):
        fl = flb[j + 2]
        state = []
        for t in range(2):
            x0, x1 = q[t, 0, j + 2], q[t, 1, j + 2]
            d0 = (x1 - x0) * oz[0, j]
            state.append([x0, x1, d0, None, None])
        for k in range(NK):
            s, b, e = sy[k, j + 1], by[k, j + 1], ey[k, j + 1]
            up = s > 0
            oy1 = oy[k, j + 3]
            if k < NK - 1:
                zs, ze = sz[k, j], ez[k, j]
                zup = zs > 0
            if k < NK - 2:
                zo = oz[k + 1, j]
            wet = fl > k
            for t in range(2):
                x, below, zd, zh, zf = state[t]
                y1, y2 = q[t, k, j + 3], q[t, k, j + 4]
                d0, h0 = dy[t, k], hy[t, k]
                d1 = (y2 - y1) * oy1
                h1 = limiter(y2 - x, d0, d1)
                f = s * x + b * d0 + e * jnp.where(up, h0, h1)
                flux = fx[slot, t, k]
                acc = (pltpu.roll(flux, 1, 1) - flux) + (fy[t, k] - f)
                if fix:
                    acc = acc + unpacked(j, NK * t + k)
                dy[t, k] = d1
                hy[t, k] = h1
                fy[t, k] = f
                if k < NK - 1:
                    if k < NK - 2:
                        deeper = q[t, k + 2, j + 2]
                        zd1 = (deeper - below) * zo
                        zh1 = limiter(deeper - x, zd, zd1)
                    else:
                        deeper, zd1, zh1 = None, None, None
                    slope_near = 0.0 if zh is None else zh
                    slope_far = 0.0 if zh1 is None else zh1
                    nf = zs * jnp.where(zup, x, below) + ze * jnp.where(zup, slope_near, slope_far)
                    acc = acc - nf
                    state[t] = [below, deeper, zd1, zh1, nf]
                if zf is not None:
                    acc = acc + zf
                if step == 0:
                    new = jnp.where(wet, x, 0.0) + acc
                else:
                    new = x + acc
                out[t, k, j + off] = new

    def sweep(q, out, off, step, first, last, repacking, fixing_in, fixing_out, at_start):
        @pl.loop(first, last)
        def _(i):
            at_start(i)

            for half in range(2):
                j = (2 * i + 2 + half) & (NJ - 1)
                if repacking:
                    repack(out, off, (j - 1) & (NJ - 1))
                rest(q, out, off, j, step, half, fixing_out)
                zonal_fluxes(q, (j + 1) & (NJ - 1), 1 - half)
                zonal_slopes(q, (j + 2) & (NJ - 1), half)
                if fixing_in:
                    add_columns(q, 2, j + 3)
                if fixing_out:
                    for n in range(3):
                        add_columns(out, off, 2 + 3 * ((j + 2) & (NJ - 1)) + n)

    def start_sweep(q):
        zonal_slopes(q, 2, 0)
        zonal_slopes(q, 3, 1)
        zonal_fluxes(q, 2, 0)
        meridional_start(q, 2)

    def restart(q):
        def at(i):
            @pl.when(i == 7)
            def _():
                meridional_start(q, 0)

        return at

    start_sweep(q0)
    sweep(q0, q1, 2, 0, 0, 8, True, False, False, restart(q0))

    for copy in own_row_copies():
        copy.wait()
    wait_rows(NORTH)

    @pl.when(low)
    def _():
        wait_rows(SOUTH)

    fold(0)
    row_static()
    row_correction(0)
    for copy in static_col_copies():
        copy.wait_recv()
    for copy in col_copies(0, 0):
        copy.wait_recv()
    edge_static()
    edge_corrections(0)
    for j in range(2, NJ - 2):
        pq[1, j] = pq[1, j] + cc[j]
    squeeze(1, range(2, NJ // 2 - 2))
    for copy in col_copies(1, 0):
        copy.start()
    add_rows(q1, 2)

    @pl.loop(0, 2)
    def _(half):
        for h in range(2):
            add_columns(q1, 2, (2 * half + h + NJ - 2) & (NJ - 1))


    def row2_copies(j, s, slot, direction, device):
        return [
            remote(
                q1.at[t, :, j + r + 2, s, :], rhal.at[1, slot, t, r],
                row2_send.at[direction, t, r], row2_recv.at[slot, t, r], device,
            )
            for t in range(2)
            for r in range(2)
        ]

    def north2(slot):
        return row2_copies(NJ - 2, NS - 1, slot, 0, north)

    def south2():
        return row2_copies(0, 0, NORTH, 1, south)

    def own2_copies():
        return [
            pltpu.make_async_copy(q1.at[t, :, j + 2, s, :], rown.at[1, t, a], own2_sem.at[t, a])
            for t in range(2)
            for a, (j, s) in enumerate(((0, 0), (1, 0), (NJ - 2, NS - 1), (NJ - 1, NS - 1)))
        ]

    for copy in north2(nslot):
        copy.start()

    @pl.when(low)
    def _():
        for copy in south2():
            copy.start()

    for copy in own2_copies():
        copy.start()

    @pl.loop(0, 2)
    def _(half):
        for h in range(2):
            repack(q1, 2, (2 * half + h + NJ - 2) & (NJ - 1))

    squeeze(1, (0, 1, NJ // 2 - 2, NJ // 2 - 1))
    for part in (1, 2):
        for copy in col_copies(1, part):
            copy.start()

    for j in (NJ - 2, NJ - 1, NJ):
        cc[j] = jnp.zeros((NS, NL), F32)
    for j in (2, 3, 4):
        add_columns(q1, 2, j)

    wrap_rows(q1)
    start_sweep(q1)

    def rows_left(i):
        @pl.when(i == 4)
        def _():
            for copy in own2_copies():
                copy.wait()
            for copy in north2(nslot):
                copy.wait_send()

    sweep(q1, ob, 0, 1, 0, 6, False, True, False, rows_left)
    for copy in north2(NORTH):
        copy.wait_recv()

    @pl.when(low)
    def _():
        for copy in north2(SOUTH):
            copy.wait_recv()

    fold(1)
    row_correction(1)
    for part in range(3):
        for copy in col_copies(1, part):
            copy.wait_recv()
    edge_corrections(1)

    OUTS = (2, 6), (8, 6), (14, 2), (0, 2)

    def out_start(part):
        first, size = OUTS[part]

        @pl.loop(0, NS)
        def _(s):
            for t, dst in enumerate((tout_hbm, sout_hbm)):
                pltpu.make_async_copy(
                    ob.at[t, :, pl.ds(first, size), s, :],
                    dst.at[:, pl.ds(NJ * s + first, size), :],
                    out_sem.at[t, part],
                ).start()

    def out_wait(part):
        first, size = OUTS[part]
        for t in range(2):
            whole = ob.at[t, :, pl.ds(first, size)]
            pltpu.make_async_copy(whole, whole, out_sem.at[t, part]).wait()

    def at_start(i):
        @pl.when(i == 7)
        def _():
            out_start(0)

        restart(q1)(i)

    sweep(q1, ob, 0, 1, 6, 8, False, False, True, at_start)
    out_start(1)
    add_rows(ob, 0)
    for part in (2, 3):
        out_start(part)

    for copy in north_rows(nslot):
        copy.wait_send()

    @pl.when(low)
    def _():
        for copy in south_rows() + south2():
            copy.wait_send()

    for copy in static_col_copies():
        copy.wait_send()
    for step in range(2):
        for part in range(len(PARTS[step])):
            for copy in col_copies(step, part):
                copy.wait_send()
    for part in range(len(OUTS)):
        out_wait(part)


def hand_over(t_in, s_in, t_out, s_out, held, in_sem, out_sem):
    pieces = [
        (src.at[pl.ds(4 * n, 4)], held.at[a, pl.ds(4 * n, 4)], dst.at[pl.ds(4 * n, 4)], a, n)
        for n in range(4)
        for a, (src, dst) in enumerate(((t_in, t_out), (s_in, s_out)))
    ]
    reads = [pltpu.make_async_copy(src, mid, in_sem.at[a, n]) for src, mid, dst, a, n in pieces]
    writes = [pltpu.make_async_copy(mid, dst, out_sem.at[a, n]) for src, mid, dst, a, n in pieces]
    for copy in reads:
        copy.start()
    for read, write in zip(reads, writes):
        read.wait()
        write.start()
    for copy in writes:
        copy.wait()


def on_device(t, s, u, v, w, kap, sea, bot):
    def vm(*lead):
        return pltpu.VMEM(lead + (NS, NL), F32)

    def rows(*lead):
        return pltpu.VMEM(lead + (NK, NL), F32)

    def vi(*lead):
        return pltpu.VMEM(lead + (NS, NL), jnp.int32)

    dma = pltpu.SemaphoreType.DMA
    anywhere = pl.BlockSpec(memory_space=pl.ANY)
    shape = jax.ShapeDtypeStruct(t.shape, F32)
    held = pl.pallas_call(
        kernel,
        out_shape=(shape, shape),
        in_specs=[anywhere] * 8,
        out_specs=(anywhere, anywhere),
        scratch_shapes=[
            vm(2, NK, NJ + 4), vm(2, NK, NJ + 4), vm(2, NK, NJ),
            vm(NK, NJ), vm(NK, NJ), vm(NK, NJ + 1), vm(NK, NJ + 2),
            vi(NJ + 4), vi(NJ + 4), vm(NJ + 4),
            vm(NK, NJ), vm(NK, NJ), vm(NK, NJ), vm(NK, NJ),
            vm(NK, NJ + 3), vm(NK, NJ + 1), vm(NK, NJ + 1), vm(NK, NJ + 1),
            vm(NK, NJ), vm(NK, NJ), vm(NK, NJ),
            vm(NK, NJ), vm(2, 2, NK), vm(2, 2, NK), vm(2, 2, NK), vm(2, NK), vm(2, NK), vm(2, NK),
            rows(2, 2, 4), rows(2, 2, 2, 2), rows(2), rows(2), rows(3), rows(2),
            pltpu.VMEM((2, 2, NL), jnp.int32), pltpu.VMEM((2, 2, NL), jnp.int32), rows(2, 7), rows(2, 4),
            vm(2, NJ), vm(2, 2, NJ // 2), vm(2, 2, NJ // 2), vm(NJ), vm(4), vm(4), vm(2), vm(2), vm(), vm(2), vm(NJ + 1),
            vm(2, NJ), vm(2, NJ), vm(2, NJ), vm(2, NJ), vm(2, NJ),
            dma((8,)), dma((13,)), dma((2, 4)), dma((2, 5)), dma((2, 8)), dma((2, 8)), dma((2, 2, 2)), dma((2, 2, 2)),
            dma((2, 2)), dma((2, 2)), dma((2, 2, 3)), dma((2, 2, 3)),
        ],
        compiler_params=pltpu.CompilerParams(
            collective_id=0, has_side_effects=True, vmem_limit_bytes=58 * 1024 * 1024
        ),
        cost_estimate=pl.CostEstimate(flops=120_000_000, bytes_accessed=9_000_000, transcendentals=0),
    )(t, s, u, v, w, kap, sea, bot)
    return pl.pallas_call(
        hand_over,
        out_shape=(shape, shape),
        in_specs=[anywhere] * 2,
        out_specs=(anywhere, anywhere),
        scratch_shapes=[pltpu.VMEM((2,) + t.shape, F32), dma((2, 4)), dma((2, 4))],
        compiler_params=pltpu.CompilerParams(vmem_limit_bytes=60 * 1024 * 1024),
    )(*held)


def solution(mesh):
    block = P(None, "ja", "ia")
    flat = P("ja", "ia")
    return jax.shard_map(
        on_device,
        mesh=mesh,
        in_specs=(block,) * 6 + (flat, flat),
        out_specs=(block, block),
        check_vma=False,
    )
```

```python
import jax
import jax.numpy as jnp
from jax import lax
from jax.experimental import pallas as pl
from jax.experimental.pallas import tpu as pltpu
from jax.sharding import PartitionSpec as P

NK = 16
NJ = 16
NS = 8
NL = 128
F32 = jnp.float32
EAST, WEST = 0, 1
SOUTH, NORTH = 0, 1


def limiter(centred, a, b):
    upper = jnp.maximum(jnp.minimum(a, b), 0.0)
    lower = jnp.minimum(jnp.maximum(a, b), 0.0)
    return jnp.maximum(jnp.minimum(centred, upper), lower)


def quarter_edge(s):
    a = jnp.abs(s)
    return a * (0.25 - 0.25 * a)


def kernel(
    t_hbm, s_hbm, u_hbm, v_hbm, w_hbm, k_hbm, sea_hbm, bot_hbm,
    tout_hbm, sout_hbm,
    q0, q1, ob, ub, wb, vb, kb, seab, botb, flb,
    ox, sx, bx, ex, oy, sy, by, ey, oz, sz, ez,
    oxw, dx, hx, fx, dy, hy, fy,
    rown, rhal, rk, rkh, rv, rvh, hs, hb, rcoef, rc,
    pq, pr, sent, uko, sent_uk, got_uk, sent_k, got_k, flo, flr, cc,
    eo, es, eb, ec, ed,
    in_sem, own_sem, own2_sem, out_sem, row_send, row_recv, row2_send, row2_recv,
    col_send, col_recv, col2_send, col2_recv,
):
    ia = lax.axis_index("ia")
    ja = lax.axis_index("ja")
    n_ia = lax.axis_size("ia")
    n_ja = lax.axis_size("ja")
    top = ja == n_ja - 1
    low = ja > 0
    east = {"ia": lax.rem(ia + 1, n_ia), "ja": ja}
    west = {"ia": lax.rem(ia + n_ia - 1, n_ia), "ja": ja}
    north = {"ia": jnp.where(top, n_ia - 1 - ia, ia), "ja": jnp.where(top, ja, ja + 1)}
    south = {"ia": ia, "ja": jnp.maximum(ja - 1, 0)}
    nslot = jnp.where(top, NORTH, SOUTH)
    mesh_ids = pl.DeviceIdType.MESH

    lane = lax.broadcasted_iota(jnp.int32, (NS, NL), 1)
    sub = lax.broadcasted_iota(jnp.int32, (NS, NL), 0)
    l4 = lane & 3
    group = lane >> 2
    edge_lanes = ((lane + 2) & (NL - 1)) < 4

    barrier = pltpu.get_barrier_semaphore()
    for device in (east, west, north):
        pl.semaphore_signal(barrier, inc=1, device_id=device, device_id_type=mesh_ids)

    @pl.when(low)
    def _():
        pl.semaphore_signal(barrier, inc=1, device_id=south, device_id_type=mesh_ids)

    @pl.loop(0, NS)
    def _(s):
        rows = pl.ds(pl.multiple_of(NJ * s, NJ), NJ)
        inner = pl.ds(2, NJ)
        inner1 = pl.ds(1, NJ)
        for index, (src, dst) in enumerate((
            (t_hbm.at[:, rows, :], q0.at[0, :, inner, s, :]),
            (s_hbm.at[:, rows, :], q0.at[1, :, inner, s, :]),
            (sea_hbm.at[rows, :], seab.at[inner, s, :]),
            (bot_hbm.at[rows, :], botb.at[inner, s, :]),
            (u_hbm.at[:, rows, :], ub.at[:, :, s, :]),
            (k_hbm.at[:, rows, :], kb.at[:, inner1, s, :]),
            (v_hbm.at[:, rows, :], vb.at[:, inner1, s, :]),
            (w_hbm.at[:, rows, :], wb.at[:, :, s, :]),
        )):
            pltpu.make_async_copy(src, dst, in_sem.at[index]).start()

    def loaded(index, whole):
        pltpu.make_async_copy(whole, whole, in_sem.at[index]).wait()

    rows_total = NJ * NS
    edge_rows = (0, 1, rows_total - 2, rows_total - 1)

    def own_row_copies():
        pairs = [
            (src.at[:, row, :], rown.at[0, t, a])
            for t, src in enumerate((t_hbm, s_hbm))
            for a, row in enumerate(edge_rows)
        ]
        pairs += [(k_hbm.at[:, row, :], rk.at[a]) for a, row in enumerate((0, rows_total - 1))]
        pairs += [(v_hbm.at[:, row, :], rv.at[a]) for a, row in enumerate((0, rows_total - 2, rows_total - 1))]
        return [pltpu.make_async_copy(a, b, own_sem.at[n]) for n, (a, b) in enumerate(pairs)]

    for copy in own_row_copies():
        copy.start()

    def remote(src, dst, ssem, rsem, device):
        return pltpu.make_async_remote_copy(
            src_ref=src, dst_ref=dst, send_sem=ssem, recv_sem=rsem,
            device_id=device, device_id_type=mesh_ids,
        )

    def row_copies(first, last, slot, direction, device):
        pair = pl.ds(first, 2)
        parts = [
            (src.at[:, first + r, :], rhal.at[0, slot, t, r])
            for t, src in enumerate((t_hbm, s_hbm))
            for r in range(2)
        ] + [
            (k_hbm.at[:, last, :], rkh.at[slot]),
            (v_hbm.at[:, last, :], rvh.at[slot]),
            (sea_hbm.at[pair, :], hs.at[slot]),
            (bot_hbm.at[pair, :], hb.at[slot]),
        ]
        return [
            remote(src, dst, row_send.at[direction, n], row_recv.at[slot, n], device)
            for n, (src, dst) in enumerate(parts)
        ]

    def north_rows(slot):
        return row_copies(rows_total - 2, rows_total - 1, slot, 0, north)

    def south_rows():
        return row_copies(0, 0, NORTH, 1, south)

    def pack(load_vreg, count):
        acc = jnp.zeros((NS, NL), F32)
        for n in range(count):
            moved = pltpu.roll(load_vreg(n), (4 * n + 2) % NL, 1)
            acc = jnp.where(group == n, moved, acc)
        return acc

    PARTS = ((0, NJ // 2),), ((2, NJ // 2 - 4), (NJ // 2 - 2, 2), (0, 2))

    def squeeze(step, rows):
        pair = lane & 63
        index = 4 * (pair >> 1) + (pair & 1)
        first = lane < NL // 2
        for a in rows:
            for side in (EAST, WEST):
                at = index + (2 if side == WEST else 0)
                sent[step, side, a] = jnp.where(
                    first,
                    jnp.take_along_axis(pq[step, a], at, axis=1),
                    jnp.take_along_axis(pq[step, a + NJ // 2], at, axis=1),
                )

    def col_copies(step, part):
        first, size = PARTS[step][part]
        sl = pl.ds(first, size)
        return [
            remote(sent.at[step, WEST, sl], pr.at[step, EAST, sl], col2_send.at[step, 0, part], col2_recv.at[step, EAST, part], west),
            remote(sent.at[step, EAST, sl], pr.at[step, WEST, sl], col2_send.at[step, 1, part], col2_recv.at[step, WEST, part], east),
        ]

    def squeeze_static():
        quarter = lane & 31
        to_east = 4 * quarter + 1
        to_west = NL // 2 + 4 * (lane & 15) + 2
        for m in range(4):
            acc = jnp.take_along_axis(uko[m], to_east, axis=1)
            for n in range(1, 4):
                acc = jnp.where((lane >> 5) == n, jnp.take_along_axis(uko[m + 4 * n], to_east, axis=1), acc)
            sent_uk[m] = acc
        for m in range(2):
            acc = jnp.take_along_axis(uko[m], to_west, axis=1)
            for n in range(1, 8):
                acc = jnp.where((lane >> 4) == n, jnp.take_along_axis(uko[m + 2 * n], to_west, axis=1), acc)
            sent_k[m] = acc

    def static_col_copies():
        return [
            remote(sent_k, got_k, col_send.at[0, 0], col_recv.at[EAST, 0], west),
            remote(sent_uk, got_uk, col_send.at[1, 0], col_recv.at[WEST, 0], east),
            remote(flo, flr.at[EAST], col_send.at[0, 1], col_recv.at[EAST, 1], west),
            remote(flo, flr.at[WEST], col_send.at[1, 1], col_recv.at[WEST, 1], east),
        ]

    loaded(0, q0.at[0, :, pl.ds(2, NJ)])
    loaded(1, q0.at[1, :, pl.ds(2, NJ)])

    @pl.loop(0, NJ // 2)
    def _(half):
        for h in range(2):
            j = 2 * half + h
            pq[0, j] = pack(lambda n: q0[n // NK, n % NK, j + 2], 2 * NK)

    loaded(2, seab.at[pl.ds(2, NJ)])
    loaded(3, botb.at[pl.ds(2, NJ)])
    for j in range(2, NJ + 2):
        flb[j] = (seab[j] * botb[j]).astype(F32)
    flo[...] = pack(lambda n: flb[n + 2], NJ)
    loaded(4, ub)
    loaded(5, kb.at[:, pl.ds(1, NJ)])

    def first_sends():
        pl.semaphore_wait(barrier, jnp.where(low, 4, 3))
        for copy in col_copies(0, 0):
            copy.start()
        for copy in north_rows(nslot):
            copy.start()

        @pl.when(low)
        def _():
            for copy in south_rows():
                copy.start()

    squeeze(0, range(NJ // 2))

    loaded(6, vb.at[:, pl.ds(1, NJ)])
    loaded(7, wb)

    def open_y(j):
        face = jnp.minimum(flb[j + 2], flb[j + 3])
        for k in range(NK):
            oy[k, j + 2] = jnp.where(face > k, 4.0, 0.0)

    def coef_y(j):
        face = jnp.minimum(flb[j + 2], flb[j + 3])
        for k in range(NK):
            v = vb[k, j + 1]
            sy[k, j + 1] = jnp.where(face > k, v, 0.0)
            by[k, j + 1] = jnp.minimum(0.25 * v, 0.0) - 0.125 * (kb[k, j + 1] + kb[k, j + 2])
            ey[k, j + 1] = quarter_edge(v)

    @pl.loop(0, NJ)
    def _(j):
        @pl.when(j == NJ // 4)
        def _():
            first_sends()

        fl = flb[j + 2]
        face = jnp.where(lane == NL - 1, 0.0, jnp.minimum(fl, pltpu.roll(fl, NL - 1, 1)))
        uko[j] = pack(lambda n: ub[n, j] if n < NK else kb[n - NK, j + 1], 2 * NK)
        face_w = jnp.where(lane == 0, 0.0, jnp.minimum(fl, pltpu.roll(fl, 1, 1)))
        for k in range(NK):
            is_open = face > k
            u = ub[k, j]
            kap = kb[k, j + 1]
            ox[k, j] = jnp.where(is_open, 4.0, 0.0)
            oxw[k, j] = jnp.where(face_w > k, 4.0, 0.0)
            sx[k, j] = jnp.where(is_open, u, 0.0)
            bx[k, j] = jnp.minimum(0.25 * u, 0.0) - 0.125 * (kap + pltpu.roll(kap, NL - 1, 1))
            ex[k, j] = quarter_edge(u)
            if k < NK - 1:
                below = fl > k + 1
                w = wb[k, j]
                oz[k, j] = jnp.where(below, 4.0, 0.0)
                sz[k, j] = jnp.where(below, w, 0.0)
                ez[k, j] = quarter_edge(w)

    squeeze_static()
    for copy in static_col_copies():
        copy.start()

    for r in range(2):
        flb[r] = jnp.where(sub == 0, 0.0, pltpu.roll(flb[NJ + r], 1, 0))
        flb[NJ + 2 + r] = jnp.where(sub == NS - 1, 0.0, pltpu.roll(flb[2 + r], NS - 1, 0))
    for k in range(NK):
        kb[k, 0] = pltpu.roll(kb[k, NJ], 1, 0)
        kb[k, NJ + 1] = pltpu.roll(kb[k, 1], NS - 1, 0)
        vb[k, 0] = pltpu.roll(vb[k, NJ], 1, 0)

    @pl.loop(0, NJ + 1)
    def _(j):
        open_y(j - 1)
        coef_y(j - 1)

    @pl.loop(0, 2)
    def _(r):
        open_y((NJ + 2) * r - 2)

    def wrap_rows(q):
        @pl.loop(0, NK // 4)
        def _(kk):
            for k4 in range(4):
                k = 4 * kk + k4
                for t in range(2):
                    for r in range(2):
                        q[t, k, r] = pltpu.roll(q[t, k, NJ + r], 1, 0)
                        q[t, k, NJ + 2 + r] = pltpu.roll(q[t, k, 2 + r], NS - 1, 0)

    wrap_rows(q0)

    def mirror(x):
        return jnp.take_along_axis(x, NL - 1 - lane, axis=1)

    def levels(kk):
        return pl.ds(NS * kk, NS)

    def fold(step):
        @pl.when(top)
        def _():
            for t in range(2):
                for kk in range(NK // NS):
                    lv = levels(kk)
                    near = mirror(rhal[step, NORTH, t, 1, lv, :])
                    far = mirror(rhal[step, NORTH, t, 0, lv, :])
                    rhal[step, NORTH, t, 0, lv, :] = near
                    rhal[step, NORTH, t, 1, lv, :] = far
            if step == 0:
                for kk in range(NK // NS):
                    rkh[NORTH, levels(kk), :] = mirror(rkh[NORTH, levels(kk), :])
                for h in (hs, hb):
                    near = mirror(jnp.broadcast_to(h[NORTH, 1:2, :], (NS, NL)))
                    far = mirror(jnp.broadcast_to(h[NORTH, 0:1, :], (NS, NL)))
                    h[NORTH, 0:1, :] = near[0:1]
                    h[NORTH, 1:2, :] = far[0:1]

    def row_static():
        def line(x):
            return jnp.broadcast_to(x, (NS, NL))

        def halo_floor(slot, r):
            return line((hs[slot, r : r + 1, :] * hb[slot, r : r + 1, :]).astype(F32))

        south_floors = [
            jnp.where(low, halo_floor(SOUTH, 0), 0.0),
            jnp.where(low, halo_floor(SOUTH, 1), 0.0),
            line(flb[2, 0:1, :]),
            line(flb[3, 0:1, :]),
        ]
        north_floors = [
            line(flb[NJ, NS - 1 : NS, :]),
            line(flb[NJ + 1, NS - 1 : NS, :]),
            halo_floor(NORTH, 0),
            halo_floor(NORTH, 1),
        ]
        for kk in range(NK // NS):
            lv = levels(kk)
            depth = (sub + NS * kk).astype(F32)
            for side, floors in ((SOUTH, south_floors), (NORTH, north_floors)):
                if side == SOUTH:
                    v = jnp.where(low, rvh[SOUTH, lv, :], 0.0)
                    ka, kc = jnp.where(low, rkh[SOUTH, lv, :], 0.0), rk[0, lv, :]
                    inner = rv[0, lv, :]
                    keep = inner > 0
                else:
                    v = rv[2, lv, :]
                    ka, kc = rk[1, lv, :], rkh[NORTH, lv, :]
                    inner = rv[1, lv, :]
                    keep = inner <= 0
                for n in range(3):
                    is_open = jnp.minimum(floors[n], floors[n + 1]) > depth
                    rcoef[side, n, lv, :] = jnp.where(is_open, 4.0, 0.0)
                    if n == 1:
                        rcoef[side, 3, lv, :] = jnp.where(is_open, v, 0.0)
                rcoef[side, 4, lv, :] = jnp.minimum(0.25 * v, 0.0) - 0.125 * (ka + kc)
                rcoef[side, 5, lv, :] = quarter_edge(v)
                rcoef[side, 6, lv, :] = jnp.where(keep, quarter_edge(inner), 0.0)

    def row_correction(step):
        for t in range(2):
            for kk in range(NK // NS):
                lv = levels(kk)
                for side in (SOUTH, NORTH):
                    own = [rown[step, t, 2 * side + r, lv, :] for r in range(2)]
                    if side == SOUTH:
                        halo = [jnp.where(low, rhal[step, SOUTH, t, r, lv, :], 0.0) for r in range(2)]
                        w = halo + own
                    else:
                        halo = [rhal[step, NORTH, t, r, lv, :] for r in range(2)]
                        w = own + halo
                    d = [(w[n + 1] - w[n]) * rcoef[side, n, lv, :] for n in range(3)]
                    h1 = limiter(w[2] - w[0], d[0], d[1])
                    h2 = limiter(w[3] - w[1], d[1], d[2])
                    s = rcoef[side, 3, lv, :]
                    f = s * w[1] + rcoef[side, 4, lv, :] * d[1] + rcoef[side, 5, lv, :] * jnp.where(s > 0, h1, h2)
                    g = rcoef[side, 6, lv, :] * (h2 if side == SOUTH else h1)
                    if side == SOUTH:
                        rc[t, 0, lv, :] = f - g
                        rc[t, 1, lv, :] = g
                    else:
                        rc[t, 2, lv, :] = -g
                        rc[t, 3, lv, :] = g - f

    def add_rows(out, off):
        @pl.loop(0, NK // 4)
        def _(kk):
            for k4 in range(4):
                k = 4 * kk + k4
                for a, (j, s) in enumerate(((0, 0), (1, 0), (NJ - 2, NS - 1), (NJ - 1, NS - 1))):
                    for t in range(2):
                        out[t, k, j + off, s : s + 1, :] = (
                            out[t, k, j + off, s : s + 1, :] + rc[t, a, pl.ds(k, 1), :]
                        )

    def wait_rows(slot):
        for copy in row_copies(0, 0, slot, 0, north):
            copy.wait_recv()

    level4 = (group & (NK - 1)).astype(F32)

    def edge_static():
        @pl.loop(0, NJ // 8)
        def _(half):
          for h in range(8):
            j = 8 * half + h
            index = 4 * j + l4

            def spread(x):
                return jnp.take_along_axis(x, index, axis=1)

            own_f, east_f, west_f = spread(flo[...]), spread(flr[EAST]), spread(flr[WEST])

            level = group & (NK - 1)
            west_uk = got_uk[j & 3]
            west_at = 32 * (j >> 2) + level
            west_u = jnp.take_along_axis(west_uk, west_at, axis=1)
            west_k = jnp.take_along_axis(west_uk, west_at + NK, axis=1)
            east_k = jnp.take_along_axis(got_k[j & 1], NK * (j >> 1) + level, axis=1)

            def halves(x):
                other = pltpu.roll(x, NL // 2, 1)
                return jnp.where(lane < NL // 2, x, other), jnp.where(lane < NL // 2, other, x)

            own_u, own_k = halves(uko[j])
            first = l4 < 2
            for side in (EAST, WEST):
                if side == EAST:
                    floor, u, kap = jnp.where(first, own_f, east_f), own_u, jnp.where(first, own_k, east_k)
                else:
                    floor, u, kap = (
                        jnp.where(first, west_f, own_f),
                        jnp.where(first, west_u, own_u),
                        jnp.where(first, west_k, own_k),
                    )
                face = jnp.minimum(floor, pltpu.roll(floor, NL - 1, 1))
                is_open = (face > level4) & (l4 < 3)
                b = jnp.minimum(0.25 * u, 0.0) - 0.125 * (kap + pltpu.roll(kap, NL - 1, 1))
                e = quarter_edge(u)
                outer = l4 == 1
                eo[side, j] = jnp.where(is_open, 4.0, 0.0)
                es[side, j] = jnp.where(is_open & outer, u, 0.0)
                eb[side, j] = jnp.where(outer, b, 0.0)
                if side == EAST:
                    c_lanes, d_lanes = outer, first
                else:
                    c_lanes, d_lanes = (l4 == 1) | (l4 == 2), outer
                ec[side, j] = jnp.where((u > 0) & c_lanes, e, 0.0)
                ed[side, j] = jnp.where((u <= 0) & d_lanes, e, 0.0)

    def edge_correction(step, j):
        own = pq[step, j]
        first = l4 < 2
        sums = []
        at = 2 * group + (lane & 1) + (NL // 2 if j >= NJ // 2 else 0)
        a = j % (NJ // 2)
        for side in (EAST, WEST):
            if side == EAST:
                win = jnp.where(first, own, jnp.take_along_axis(pr[step, EAST, a], at, axis=1))
            else:
                win = jnp.where(first, jnp.take_along_axis(pr[step, WEST, a], at, axis=1), own)
            d = (pltpu.roll(win, NL - 1, 1) - win) * eo[side, j]
            before = pltpu.roll(d, 1, 1)
            h = limiter(0.25 * (d + before), before, d)
            g = es[side, j] * win + eb[side, j] * d + ec[side, j] * h + ed[side, j] * pltpu.roll(h, NL - 1, 1)
            sums.append(pltpu.roll(g, 1, 1) - g)
        cc[j] = jnp.where(first, sums[EAST], sums[WEST])

    def edge_corrections(step):
        for j in range(NJ):
            edge_correction(step, j)

    def unpacked(j, n):
        return jnp.where(edge_lanes, pltpu.roll(cc[j], (NL - 2 - 4 * n) % NL, 1), 0.0)

    def add_columns(out, off, j):
        for t in range(2):
            for k in range(NK):
                out[t, k, j + off] = out[t, k, j + off] + unpacked(j, NK * t + k)

    def zonal_slopes(q, j, slot):
        for k in range(NK):
            o, ow = ox[k, j], oxw[k, j]
            for t in range(2):
                x = q[t, k, j + 2]
                after = pltpu.roll(x, NL - 1, 1)
                before = pltpu.roll(x, 1, 1)
                d = (after - x) * o
                dx[slot, t, k] = d
                hx[slot, t, k] = limiter(after - before, (x - before) * ow, d)

    def zonal_fluxes(q, j, slot):
        for k in range(NK):
            s, b, e = sx[k, j], bx[k, j], ex[k, j]
            up = s > 0
            for t in range(2):
                x, d, h = q[t, k, j + 2], dx[slot, t, k], hx[slot, t, k]
                fx[slot, t, k] = s * x + b * d + e * jnp.where(up, h, pltpu.roll(h, NL - 1, 1))

    def repack(out, off, j):
        sums = []
        for t in range(2):
            for k in range(NK):
                n = NK * t + k
                moved = pltpu.roll(jnp.where(edge_lanes, out[t, k, j + off], 0.0), (4 * n + 2) % NL, 1)
                if len(sums) < 4:
                    sums.append(moved)
                else:
                    sums[n % 4] = sums[n % 4] + moved
        pq[1, j] = (sums[0] + sums[1]) + (sums[2] + sums[3])

    def meridional_start(q, j):
        @pl.loop(0, NK // 8)
        def _(kk):
            for k4 in range(8):
                k = 8 * kk + k4
                s, b, e = sy[k, j], by[k, j], ey[k, j]
                for t in range(2):
                    a2, a1, c0, c1 = (q[t, k, j + n] for n in range(4))
                    d2 = (a1 - a2) * oy[k, j]
                    d1 = (c0 - a1) * oy[k, j + 1]
                    d0 = (c1 - c0) * oy[k, j + 2]
                    h1 = limiter(c0 - a2, d2, d1)
                    h0 = limiter(c1 - a1, d1, d0)
                    dy[t, k] = d0
                    hy[t, k] = h0
                    fy[t, k] = s * a1 + b * d1 + e * jnp.where(s > 0, h1, h0)

    def rest(q, out, off, j, step, slot, fix):
        fl = flb[j + 2]
        state = []
        for t in range(2):
            x0, x1 = q[t, 0, j + 2], q[t, 1, j + 2]
            d0 = (x1 - x0) * oz[0, j]
            state.append([x0, x1, d0, None, None])
        for k in range(NK):
            s, b, e = sy[k, j + 1], by[k, j + 1], ey[k, j + 1]
            up = s > 0
            oy1 = oy[k, j + 3]
            if k < NK - 1:
                zs, ze = sz[k, j], ez[k, j]
                zup = zs > 0
            if k < NK - 2:
                zo = oz[k + 1, j]
            wet = fl > k
            for t in range(2):
                x, below, zd, zh, zf = state[t]
                y1, y2 = q[t, k, j + 3], q[t, k, j + 4]
                d0, h0 = dy[t, k], hy[t, k]
                d1 = (y2 - y1) * oy1
                h1 = limiter(y2 - x, d0, d1)
                f = s * x + b * d0 + e * jnp.where(up, h0, h1)
                flux = fx[slot, t, k]
                acc = (pltpu.roll(flux, 1, 1) - flux) + (fy[t, k] - f)
                if fix:
                    acc = acc + unpacked(j, NK * t + k)
                dy[t, k] = d1
                hy[t, k] = h1
                fy[t, k] = f
                if k < NK - 1:
                    if k < NK - 2:
                        deeper = q[t, k + 2, j + 2]
                        zd1 = (deeper - below) * zo
                        zh1 = limiter(deeper - x, zd, zd1)
                    else:
                        deeper, zd1, zh1 = None, None, None
                    slope_near = 0.0 if zh is None else zh
                    slope_far = 0.0 if zh1 is None else zh1
                    nf = zs * jnp.where(zup, x, below) + ze * jnp.where(zup, slope_near, slope_far)
                    acc = acc - nf
                    state[t] = [below, deeper, zd1, zh1, nf]
                if zf is not None:
                    acc = acc + zf
                if step == 0:
                    new = jnp.where(wet, x, 0.0) + acc
                else:
                    new = x + acc
                out[t, k, j + off] = new

    def sweep(q, out, off, step, first, last, repacking, fixing_in, fixing_out, at_start):
        @pl.loop(first, last)
        def _(i):
            at_start(i)

            for half in range(2):
                j = (2 * i + 2 + half) & (NJ - 1)
                if repacking:
                    repack(out, off, (j - 1) & (NJ - 1))
                rest(q, out, off, j, step, half, fixing_out)
                zonal_fluxes(q, (j + 1) & (NJ - 1), 1 - half)
                zonal_slopes(q, (j + 2) & (NJ - 1), half)
                if fixing_in:
                    add_columns(q, 2, j + 3)
                if fixing_out:
                    for n in range(3):
                        add_columns(out, off, 2 + 3 * ((j + 2) & (NJ - 1)) + n)

    def start_sweep(q):
        zonal_slopes(q, 2, 0)
        zonal_slopes(q, 3, 1)
        zonal_fluxes(q, 2, 0)
        meridional_start(q, 2)

    def restart(q):
        def at(i):
            @pl.when(i == 7)
            def _():
                meridional_start(q, 0)

        return at

    start_sweep(q0)
    sweep(q0, q1, 2, 0, 0, 8, True, False, False, restart(q0))

    for copy in own_row_copies():
        copy.wait()
    wait_rows(NORTH)

    @pl.when(low)
    def _():
        wait_rows(SOUTH)

    fold(0)
    row_static()
    row_correction(0)
    for copy in static_col_copies():
        copy.wait_recv()
    for copy in col_copies(0, 0):
        copy.wait_recv()
    edge_static()
    edge_corrections(0)
    for j in range(2, NJ - 2):
        pq[1, j] = pq[1, j] + cc[j]
    squeeze(1, range(2, NJ // 2 - 2))
    for copy in col_copies(1, 0):
        copy.start()
    add_rows(q1, 2)

    @pl.loop(0, 2)
    def _(half):
        for h in range(2):
            add_columns(q1, 2, (2 * half + h + NJ - 2) & (NJ - 1))


    def row2_copies(j, s, slot, direction, device):
        return [
            remote(
                q1.at[t, :, j + r + 2, s, :], rhal.at[1, slot, t, r],
                row2_send.at[direction, t, r], row2_recv.at[slot, t, r], device,
            )
            for t in range(2)
            for r in range(2)
        ]

    def north2(slot):
        return row2_copies(NJ - 2, NS - 1, slot, 0, north)

    def south2():
        return row2_copies(0, 0, NORTH, 1, south)

    def own2_copies():
        return [
            pltpu.make_async_copy(q1.at[t, :, j + 2, s, :], rown.at[1, t, a], own2_sem.at[t, a])
            for t in range(2)
            for a, (j, s) in enumerate(((0, 0), (1, 0), (NJ - 2, NS - 1), (NJ - 1, NS - 1)))
        ]

    for copy in north2(nslot):
        copy.start()

    @pl.when(low)
    def _():
        for copy in south2():
            copy.start()

    for copy in own2_copies():
        copy.start()

    @pl.loop(0, 2)
    def _(half):
        for h in range(2):
            repack(q1, 2, (2 * half + h + NJ - 2) & (NJ - 1))

    squeeze(1, (0, 1, NJ // 2 - 2, NJ // 2 - 1))
    for part in (1, 2):
        for copy in col_copies(1, part):
            copy.start()

    for j in (NJ - 2, NJ - 1, NJ):
        cc[j] = jnp.zeros((NS, NL), F32)
    for j in (2, 3, 4):
        add_columns(q1, 2, j)

    wrap_rows(q1)
    start_sweep(q1)

    def rows_left(i):
        @pl.when(i == 4)
        def _():
            for copy in own2_copies():
                copy.wait()
            for copy in north2(nslot):
                copy.wait_send()

    sweep(q1, ob, 0, 1, 0, 6, False, True, False, rows_left)
    for copy in north2(NORTH):
        copy.wait_recv()

    @pl.when(low)
    def _():
        for copy in north2(SOUTH):
            copy.wait_recv()

    fold(1)
    row_correction(1)
    for part in range(3):
        for copy in col_copies(1, part):
            copy.wait_recv()
    edge_corrections(1)

    OUTS = (2, 6), (8, 6), (14, 2), (0, 2)

    def out_start(part):
        first, size = OUTS[part]

        @pl.loop(0, NS)
        def _(s):
            for t, dst in enumerate((tout_hbm, sout_hbm)):
                pltpu.make_async_copy(
                    ob.at[t, :, pl.ds(first, size), s, :],
                    dst.at[:, pl.ds(NJ * s + first, size), :],
                    out_sem.at[t, part],
                ).start()

    def out_wait(part):
        first, size = OUTS[part]
        for t in range(2):
            whole = ob.at[t, :, pl.ds(first, size)]
            pltpu.make_async_copy(whole, whole, out_sem.at[t, part]).wait()

    def at_start(i):
        @pl.when(i == 7)
        def _():
            out_start(0)

        restart(q1)(i)

    sweep(q1, ob, 0, 1, 6, 8, False, False, True, at_start)
    out_start(1)
    add_rows(ob, 0)
    for part in (2, 3):
        out_start(part)

    for copy in north_rows(nslot):
        copy.wait_send()

    @pl.when(low)
    def _():
        for copy in south_rows() + south2():
            copy.wait_send()

    for copy in static_col_copies():
        copy.wait_send()
    for step in range(2):
        for part in range(len(PARTS[step])):
            for copy in col_copies(step, part):
                copy.wait_send()
    for part in range(len(OUTS)):
        out_wait(part)


def hand_over(t_in, s_in, t_out, s_out, held, in_sem, out_sem):
    pieces = [
        (src.at[pl.ds(8 * n, 8)], held.at[a, pl.ds(8 * n, 8)], dst.at[pl.ds(8 * n, 8)], a, n)
        for n in range(2)
        for a, (src, dst) in enumerate(((t_in, t_out), (s_in, s_out)))
    ]
    reads = [pltpu.make_async_copy(src, mid, in_sem.at[a, n]) for src, mid, dst, a, n in pieces]
    writes = [pltpu.make_async_copy(mid, dst, out_sem.at[a, n]) for src, mid, dst, a, n in pieces]
    for copy in reads:
        copy.start()
    for read, write in zip(reads, writes):
        read.wait()
        write.start()
    for copy in writes:
        copy.wait()


def on_device(t, s, u, v, w, kap, sea, bot):
    def vm(*lead):
        return pltpu.VMEM(lead + (NS, NL), F32)

    def rows(*lead):
        return pltpu.VMEM(lead + (NK, NL), F32)

    def vi(*lead):
        return pltpu.VMEM(lead + (NS, NL), jnp.int32)

    dma = pltpu.SemaphoreType.DMA
    anywhere = pl.BlockSpec(memory_space=pl.ANY)
    shape = jax.ShapeDtypeStruct(t.shape, F32)
    held = pl.pallas_call(
        kernel,
        out_shape=(shape, shape),
        in_specs=[anywhere] * 8,
        out_specs=(anywhere, anywhere),
        scratch_shapes=[
            vm(2, NK, NJ + 4), vm(2, NK, NJ + 4), vm(2, NK, NJ),
            vm(NK, NJ), vm(NK, NJ), vm(NK, NJ + 1), vm(NK, NJ + 2),
            vi(NJ + 4), vi(NJ + 4), vm(NJ + 4),
            vm(NK, NJ), vm(NK, NJ), vm(NK, NJ), vm(NK, NJ),
            vm(NK, NJ + 3), vm(NK, NJ + 1), vm(NK, NJ + 1), vm(NK, NJ + 1),
            vm(NK, NJ), vm(NK, NJ), vm(NK, NJ),
            vm(NK, NJ), vm(2, 2, NK), vm(2, 2, NK), vm(2, 2, NK), vm(2, NK), vm(2, NK), vm(2, NK),
            rows(2, 2, 4), rows(2, 2, 2, 2), rows(2), rows(2), rows(3), rows(2),
            pltpu.VMEM((2, 2, NL), jnp.int32), pltpu.VMEM((2, 2, NL), jnp.int32), rows(2, 7), rows(2, 4),
            vm(2, NJ), vm(2, 2, NJ // 2), vm(2, 2, NJ // 2), vm(NJ), vm(4), vm(4), vm(2), vm(2), vm(), vm(2), vm(NJ + 1),
            vm(2, NJ), vm(2, NJ), vm(2, NJ), vm(2, NJ), vm(2, NJ),
            dma((8,)), dma((13,)), dma((2, 4)), dma((2, 5)), dma((2, 8)), dma((2, 8)), dma((2, 2, 2)), dma((2, 2, 2)),
            dma((2, 2)), dma((2, 2)), dma((2, 2, 3)), dma((2, 2, 3)),
        ],
        compiler_params=pltpu.CompilerParams(
            collective_id=0, has_side_effects=True, vmem_limit_bytes=58 * 1024 * 1024
        ),
        cost_estimate=pl.CostEstimate(flops=120_000_000, bytes_accessed=9_000_000, transcendentals=0),
    )(t, s, u, v, w, kap, sea, bot)
    return pl.pallas_call(
        hand_over,
        out_shape=(shape, shape),
        in_specs=[anywhere] * 2,
        out_specs=(anywhere, anywhere),
        scratch_shapes=[pltpu.VMEM((2,) + t.shape, F32), dma((2, 4)), dma((2, 4))],
        compiler_params=pltpu.CompilerParams(vmem_limit_bytes=60 * 1024 * 1024),
    )(*held)


def solution(mesh):
    block = P(None, "ja", "ia")
    flat = P("ja", "ia")
    return jax.shard_map(
        on_device,
        mesh=mesh,
        in_specs=(block,) * 6 + (flat, flat),
        out_specs=(block, block),
        check_vma=False,
    )
```
